512 devices in a mesh: slab: 32 (over y, x, core), tile: 16 (over z).
Axes of the slice: x: 4, y: 4, z: 16, core: 2. Of those that a mesh axis runs over, the one named last changes fastest.
Arguments:
- history: bfloat16 [32, 2048, 8, 128], P('slab', 'tile'), may hold values from -15 to 15
- positions: bfloat16 [32, 2048, 3, 128], P('slab', 'tile'), may hold values from 0 to 1
- kappa_old: float32 [32, 2048, 128], P('slab', 'tile'), may hold values from 0.2 to 2
- threshold: float32 [32, 2048, 128], P('slab', 'tile'), may hold values from 0.3 to 1.5
- pair_ids: int32 [32, 2048, 8], P('slab', 'tile'), may hold values from 0 to 2047, as said below
- reader_counts: int32 [32, 2048], P('slab', 'tile'), may hold values from 1 to 8, as said below
- brick_map: int32 [32, 2048], P('slab', 'tile'), may hold values from 0 to 511, as said below
- strain_disp: bfloat16 [1024, 128], replicated, may hold values from -0.1875 to 0.1875
- couple: float32 [128, 128], replicated, may hold values from -0.5 to 0.5
Outputs:
- damage: float32 [32, 2048, 128], P('slab', 'tile')
- residual: float32 [1024, 16, 128], P('slab', 'tile')
The draws below stay inside these ranges and needn't reach their ends.
Inputs may be any that keep to these rules, and one draw needn't show every extreme that they name: pair_ids[s, r, 0] = r; the other sources may be any clusters of the same depth layer. Only the first reader_counts[s, r] entries of pair_ids[s, r] are used. `brick_map`: a cluster among clusters t * 128 to (t + 1) * 128 - 1 lies in a brick among bricks (t - 1) * 32 to (t + 2) * 32 - 1.
All inputs are finite; a program needn't handle non-finite values.
Results may differ from the reference program's by a relative error of at most 0.0054.
Values may be sent and summed in bfloat16 or wider, within the bound.
No kernel may reach another device: no remote copies, remote signals or barrier semaphores. Data moves between devices by JAX's collectives and lax.ppermute only.
A program may use at most 64 MiB of HBM per device.

```python
import math
import jax
import jax.numpy as jnp
from jax import lax

PTS = 128
COLS = 8
DOF = 128
PAIRS = 8
CL_DEV = 128
BR_DEV = 32
SLABS = 32
CL_ROW = 2048
BR_ROW = 512
BR_DEPTH = 1024
N_TILE = 16


def draw_pair_ids(key, part):
    tiles = CL_ROW // CL_DEV
    rows = jnp.arange(CL_ROW, dtype=jnp.int32)
    tile_of = rows // CL_DEV
    shape = (SLABS, CL_ROW, PAIRS)
    ids = jax.random.randint(jax.random.fold_in(key, 11), shape, 0, CL_ROW, dtype=jnp.int32)
    far_local = jax.random.randint(jax.random.fold_in(key, 13), (SLABS, CL_ROW), 0, CL_DEV, dtype=jnp.int32)
    far_tile = (tile_of[None, :] + tiles // 2) % tiles
    far_ids = far_tile * CL_DEV + far_local
    entry = jnp.arange(PAIRS, dtype=jnp.int32)[None, None, :]
    first_row = (rows % CL_DEV == 0)[None, :, None]
    ids = jnp.where(first_row & (entry == 1), far_ids[:, :, None], ids)
    own = jnp.broadcast_to(rows[None, :, None], shape)
    return jnp.where(entry == 0, own, ids).astype(jnp.int32)


def draw_reader_counts(key, part):
    layer = jnp.arange(SLABS, dtype=jnp.int32)[:, None]
    rows = jnp.arange(CL_ROW, dtype=jnp.int32)[None, :]
    top = 1 + ((PAIRS - 1) * (SLABS - layer) + SLABS - 1) // SLABS
    top = jnp.broadcast_to(top, (SLABS, CL_ROW))
    counts = jax.random.randint(jax.random.fold_in(key, 23), (SLABS, CL_ROW), 1, top + 1, dtype=jnp.int32)
    return jnp.where(rows % CL_DEV == 0, PAIRS, counts).astype(jnp.int32)


def draw_brick_map(key, part):
    tiles = CL_ROW // CL_DEV
    rows = jnp.arange(CL_ROW, dtype=jnp.int32)
    tile_of = (rows // CL_DEV)[None, :]
    key_off, key_loc = jax.random.split(jax.random.fold_in(key, 37))
    offset = jax.random.randint(key_off, (SLABS, CL_ROW), -1, 2, dtype=jnp.int32)
    target = jnp.clip(tile_of + offset, 0, tiles - 1)
    local = jax.random.randint(key_loc, (SLABS, CL_ROW), 0, BR_DEV, dtype=jnp.int32)
    return (target * BR_DEV + local).astype(jnp.int32)


def block_scale(key, extent, shards, low, top_value):
    loudness = 1.0
    for dim, shards_of in shards:
        draws = jax.random.uniform(jax.random.fold_in(jax.random.fold_in(key, 6), dim), (shards_of,), jnp.float32, low / len(shards), top_value / len(shards))
        loudness = loudness * jnp.repeat(jnp.exp(draws), extent[dim] // shards_of).reshape((-1,) + (1,) * (len(extent) - 1 - dim))
    return loudness


def normal_values(key, shape, width, limit, pieces=(), kind=jnp.bfloat16):
    array = jax.random.normal(key, shape, jnp.float32) * width
    if len(pieces) > 0:
        array = block_scale(key, shape, pieces, -0.22, 0.18) * array
    return jnp.clip(array, min=-limit, max=limit).astype(kind)


def setup_inputs(seed: int = 0) -> dict:
    streams_of = jax.random.split(jax.random.key(seed), 10)
    history = normal_values(streams_of[0], (SLABS, CL_ROW, COLS, PTS), 3.0, 15.0, ((0, 32), (1, 16)))
    positions = jnp.clip(1.0 * jax.random.uniform(streams_of[1], (SLABS, CL_ROW, 3, PTS), jnp.float32) ** block_scale(streams_of[1], (SLABS, CL_ROW, 3, PTS), ((0, 32), (1, 16)), -0.2, 0.2), 0.0, 1.0).astype(jnp.bfloat16)
    kappa_old = jnp.clip(jnp.exp(math.log(2.0) - 2.3025851 * jax.random.uniform(streams_of[2], (SLABS, CL_ROW, PTS), jnp.float32) ** block_scale(streams_of[2], (SLABS, CL_ROW, PTS), ((0, 32), (1, 16)), -0.2, 0.2)), 0.2, 2.0)
    threshold = jnp.clip(jnp.exp(math.log(1.5) - 1.60943787 * jax.random.uniform(streams_of[3], (SLABS, CL_ROW, PTS), jnp.float32) ** block_scale(streams_of[3], (SLABS, CL_ROW, PTS), ((0, 32), (1, 16)), -0.2, 0.2)), 0.3, 1.5)
    pair_ids = draw_pair_ids(jax.random.fold_in(streams_of[9], 71), 0)
    reader_counts = draw_reader_counts(jax.random.fold_in(streams_of[9], 71), 0)
    brick_map = draw_brick_map(jax.random.fold_in(streams_of[9], 71), 0)
    strain_disp = normal_values(streams_of[7], (COLS * PTS, DOF), (COLS * PTS) ** -0.5, 0.1875)
    couple = normal_values(streams_of[8], (DOF, DOF), DOF ** -0.5, 0.5, (), jnp.float32)
    return {"history": history, "positions": positions, "kappa_old": kappa_old, "threshold": threshold, "pair_ids": pair_ids, "reader_counts": reader_counts, "brick_map": brick_map, "strain_disp": strain_disp, "couple": couple}


SHARP = 12.0
SOFTEN = 2.0


def reference(history, positions, kappa_old, threshold, pair_ids, reader_counts, brick_map, strain_disp, couple):
    def one_slab(inputs):
        hist_layer, pos_layer, ids_layer, count_layer = inputs

        def one_reader(pos_here, ids_here, count_here):
            here = pos_here.astype(jnp.float32)
            numer = jnp.zeros((COLS, PTS), jnp.float32)
            denom = jnp.zeros((PTS,), jnp.float32)
            for entry in range(PAIRS):
                source = ids_here[entry]
                src_hist = hist_layer[source]
                src_pos = pos_layer[source].astype(jnp.float32)
                dist = jnp.zeros((PTS, PTS), jnp.float32)
                for axis_k in range(3):
                    delta = here[axis_k][:, None] - src_pos[axis_k][None, :]
                    dist = dist + delta * delta
                live = (entry < count_here).astype(jnp.float32)
                weight = (jnp.exp(-SHARP * dist) * live).astype(jnp.bfloat16)
                numer = numer + jnp.dot(src_hist, weight.T, preferred_element_type=jnp.float32)
                denom = denom + jnp.sum(weight.astype(jnp.float32), axis=1)
            return numer / denom[None, :]

        return jax.vmap(one_reader)(pos_layer, ids_layer, count_layer)

    averaged = lax.map(one_slab, (history, positions, pair_ids, reader_counts))
    kappa = jnp.maximum(jnp.maximum(kappa_old, averaged[:, :, 0, :]), threshold)
    damage = 1.0 - (threshold / kappa) * jnp.exp(-(kappa - threshold) / SOFTEN)
    effective = ((1.0 - damage)[:, :, None, :] * averaged).astype(jnp.bfloat16)
    term = jnp.dot(effective.reshape(-1, COLS * PTS), strain_disp, preferred_element_type=jnp.float32)
    term = term.reshape(SLABS, CL_ROW, DOF)
    brick_force = jax.vmap(lambda t, m: jax.ops.segment_sum(t, m, num_segments=BR_ROW))(term, brick_map)
    force = brick_force.reshape(SLABS, N_TILE, BR_DEV, DOF).transpose(0, 2, 1, 3).reshape(BR_DEPTH, N_TILE, DOF)
    padded = jnp.pad(force, ((1, 1), (0, 0), (0, 0)))
    beside = padded[:-2] + padded[2:]
    coupled = jnp.dot(beside.reshape(-1, DOF), couple, precision=lax.Precision.HIGHEST, preferred_element_type=jnp.float32)
    residual = force + coupled.reshape(BR_DEPTH, N_TILE, DOF)
    return damage, residual
```

```python
import functools
import math

import jax
import jax.numpy as jnp
from jax import lax
from jax.experimental import pallas as pl
from jax.experimental.pallas import tpu as pltpu
from jax.sharding import PartitionSpec as P

PTS = 128
COLS = 8
PAIRS = 8
CL = 128
BR_DEV = 32
N_TILE = 16
SHARP = 12.0
SOFTEN = 2.0
SCALE = SHARP * math.log2(math.e)

UNITS = 4
STEP = 2 * UNITS
KDIM = 16
MAX_STEPS = (CL * PAIRS + N_TILE * (STEP - 1)) // STEP
LISTED = MAX_STEPS * STEP
HIST_ROWS = CL * COLS
ACC_ROWS = (CL + 1) * 2 * COLS


def list_kernel(ids_ref, cnt_ref, tile_ref, here_ref, r_ref, q_ref, meta_ref, x_ref, cur_ref, rows_ref):
    reader_rows(here_ref, rows_ref, x_ref)
    tile = tile_ref[0]
    for c in range(N_TILE):
        cur_ref[c] = 0

    def count_reader(r, carry):
        def count_entry(p, carry):
            c = ((ids_ref[p, r] >> 7) - tile) & (N_TILE - 1)
            cur_ref[c] = cur_ref[c] + 1
            return carry

        return lax.fori_loop(0, cnt_ref[0, r], count_entry, carry)

    lax.fori_loop(0, CL, count_reader, 0)
    start = jnp.int32(0)
    ends = []
    for c in range(N_TILE):
        meta_ref[c] = start
        at = start * STEP
        start = start + ((cur_ref[c] + (STEP - 1)) >> 3)
        cur_ref[c] = at
        ends.append(start * STEP)
    meta_ref[N_TILE] = start
    meta_ref[N_TILE + 1] = tile

    def fill_reader(r, carry):
        def fill_entry(p, carry):
            q = ids_ref[p, r]
            c = ((q >> 7) - tile) & (N_TILE - 1)
            at = cur_ref[c]
            r_ref[at] = r
            q_ref[at] = q & (CL - 1)
            cur_ref[c] = at + 1
            return carry

        return lax.fori_loop(0, cnt_ref[0, r], fill_entry, carry)

    lax.fori_loop(0, CL, fill_reader, 0)
    for c in range(N_TILE):

        def pad(at, carry):
            r_ref[at] = CL
            q_ref[at] = 0
            return carry

        lax.fori_loop(cur_ref[c], ends[c], pad, 0)


def reader_rows(here_ref, rows_ref, x_ref):
    here = [here_ref[k].astype(jnp.float32) for k in range(3)]
    twice = [split3((2.0 * SCALE) * h) for h in here]
    norm = split3(-SCALE * (here[0] * here[0] + here[1] * here[1] + here[2] * here[2]))
    rows = [twice[k][t] for t in range(3) for k in range(3)] + list(norm)
    rows_ref[...] = jnp.ones_like(rows_ref)
    for k, row in enumerate(rows):
        rows_ref[pl.ds(k, CL, stride=KDIM), :] = row
    rows_ref[pl.ds(KDIM - 1, CL, stride=KDIM), :] = jnp.zeros((CL, PTS), jnp.float32)

    def turn(r, carry):
        rows = rows_ref[pl.ds(pl.multiple_of(r * KDIM, KDIM), KDIM), :]
        x_ref[r] = jnp.concatenate([rows, rows], axis=0).T.astype(jnp.bfloat16)
        return carry

    lax.fori_loop(0, CL, turn, 0)


SMEM = pl.BlockSpec(memory_space=pltpu.SMEM)
VMEM = pl.BlockSpec(memory_space=pltpu.VMEM)


def make_lists(ids, counts, tile, here):
    return pl.pallas_call(
        list_kernel,
        out_shape=[
            jax.ShapeDtypeStruct((LISTED,), jnp.int32),
            jax.ShapeDtypeStruct((LISTED,), jnp.int32),
            jax.ShapeDtypeStruct((N_TILE + 2,), jnp.int32),
            jax.ShapeDtypeStruct((CL, PTS, 2 * KDIM), jnp.bfloat16),
        ],
        in_specs=[SMEM] * 3 + [VMEM],
        out_specs=[SMEM] * 3 + [VMEM],
        scratch_shapes=[
            pltpu.SMEM((N_TILE,), jnp.int32),
            pltpu.VMEM((CL * KDIM, PTS), jnp.float32),
        ],
        compiler_params=pltpu.CompilerParams(vmem_limit_bytes=16 * 2**20),
        cost_estimate=pl.CostEstimate(flops=10**6, bytes_accessed=5 * 10**6, transcendentals=0),
    )(ids, counts, tile, here)


def split3(x):
    hi = x.astype(jnp.bfloat16).astype(jnp.float32)
    mid = (x - hi).astype(jnp.bfloat16).astype(jnp.float32)
    return hi, mid, x - hi - mid


def prepare(source, d, hist_ref, y_ref):
    hist_ref[...] = source[d, :HIST_ROWS].astype(jnp.float32)
    at = HIST_ROWS
    spots = [source[d, at + k * CL : at + (k + 1) * CL].astype(jnp.float32) for k in range(3)]
    norm = spots[0] * spots[0] + spots[1] * spots[1] + spots[2] * spots[2]
    rows = spots * 3 + [None] * 3 + list(split3(-SCALE * norm))
    for k, row in enumerate(rows):
        if row is not None:
            y_ref[pl.ds(k, CL, stride=KDIM), :] = row


def constant_rows(y_ref):
    y_ref[...] = jnp.ones_like(y_ref)
    y_ref[pl.ds(KDIM - 1, CL, stride=KDIM), :] = jnp.zeros((CL, PTS), jnp.float32)


def pairs(begin, end, r_s, q_s, x_ref, hist_ref, y_ref, acc_ref):
    first = lax.broadcasted_iota(jnp.int32, (PTS, 2 * KDIM), 1) < KDIM
    zero_y = jnp.zeros((KDIM, PTS), jnp.float32)
    zero_h = jnp.zeros((COLS, PTS), jnp.float32)
    row = lax.broadcasted_iota(jnp.int32, (2 * COLS, 2 * PTS), 0) >> 3
    side = lax.broadcasted_iota(jnp.int32, (2 * COLS, 2 * PTS), 1) >> 7
    ones = (row == side).astype(jnp.float32).astype(jnp.bfloat16)

    def beside(one, other, zero):
        top = jnp.concatenate([one, zero], axis=1)
        bottom = jnp.concatenate([zero, other], axis=1)
        return jnp.concatenate([top, bottom], axis=0).astype(jnp.bfloat16)

    def step(i, carry):
        outs = []
        for u in range(UNITS):
            r = [r_s[i * STEP + 2 * u + k] for k in range(2)]
            q = [q_s[i * STEP + 2 * u + k] for k in range(2)]
            lhs = jnp.where(first, x_ref[r[0] & (CL - 1)], x_ref[r[1] & (CL - 1)])
            ys = [y_ref[pl.ds(pl.multiple_of(k * KDIM, KDIM), KDIM), :] for k in q]
            power = jnp.dot(lhs, beside(*ys, zero_y), preferred_element_type=jnp.float32)
            weight = jnp.exp2(power).astype(jnp.bfloat16)
            hs = [hist_ref[pl.ds(pl.multiple_of(k * COLS, COLS), COLS), :] for k in q]
            both = jnp.concatenate([beside(*hs, zero_h), ones], axis=0)
            out = lax.dot_general(
                both, weight, (((1,), (1,)), ((), ())), preferred_element_type=jnp.float32
            )
            outs.append((r, out))
        for r, out in outs:
            for half in range(2):
                at = pl.multiple_of(r[half] * (2 * COLS), 2 * COLS)
                acc_ref[pl.ds(at, COLS), :] += out[half * COLS : (half + 1) * COLS]
                acc_ref[pl.ds(at + COLS, COLS), :] += out[(2 + half) * COLS : (3 + half) * COLS]
        return carry

    lax.fori_loop(begin, end, step, 0)


def finish(acc_ref, kappa_ref, threshold_ref, disp_ref, brick_ref, damage_ref, shares_ref):
    inverse = 1.0 / acc_ref[pl.ds(COLS, CL, stride=2 * COLS), :]
    threshold = threshold_ref[...]
    strain = acc_ref[pl.ds(0, CL, stride=2 * COLS), :] * inverse
    kappa = jnp.maximum(jnp.maximum(kappa_ref[...], strain), threshold)
    damage = 1.0 - (threshold / kappa) * jnp.exp(-(kappa - threshold) / SOFTEN)
    damage_ref[...] = damage
    left = 1.0 - damage
    term = jnp.zeros((CL, PTS), jnp.float32)
    for c in range(COLS):
        mean = acc_ref[pl.ds(c, CL, stride=2 * COLS), :] * inverse
        term = term + jnp.dot(
            (left * mean).astype(jnp.bfloat16),
            disp_ref[c * PTS : (c + 1) * PTS, :],
            preferred_element_type=jnp.float32,
        )
    rows = lax.broadcasted_iota(jnp.int32, (3 * BR_DEV, CL), 0)
    onehot = (rows == brick_ref[...]).astype(jnp.float32)
    shares_ref[...] = jnp.dot(
        onehot, term, precision=lax.Precision.HIGHEST, preferred_element_type=jnp.float32
    )


def gather_kernel(
    meta,
    r_s,
    q_s,
    x_ref,
    source,
    kappa_ref,
    threshold_ref,
    disp_ref,
    brick_ref,
    damage_ref,
    shares_ref,
    acc_ref,
    hist_ref,
    y_ref,
):
    acc_ref[...] = jnp.zeros_like(acc_ref)
    constant_rows(y_ref)

    def block(rel, carry):
        prepare(source, (meta[N_TILE + 1] + rel) & (N_TILE - 1), hist_ref, y_ref)
        pairs(meta[rel], meta[rel + 1], r_s, q_s, x_ref, hist_ref, y_ref, acc_ref)
        return carry

    lax.fori_loop(0, N_TILE, block, 0)
    finish(acc_ref, kappa_ref, threshold_ref, disp_ref, brick_ref, damage_ref, shares_ref)


def consume(lists, source, final):
    r_list, q_list, meta, x_rows = lists
    return pl.pallas_call(
        gather_kernel,
        out_shape=[
            jax.ShapeDtypeStruct((CL, PTS), jnp.float32),
            jax.ShapeDtypeStruct((3 * BR_DEV, PTS), jnp.float32),
        ],
        in_specs=[SMEM] * 3 + [VMEM] * 6,
        out_specs=[VMEM] * 2,
        scratch_shapes=[
            pltpu.VMEM((ACC_ROWS, PTS), jnp.float32),
            pltpu.VMEM((HIST_ROWS, PTS), jnp.float32),
            pltpu.VMEM((CL * KDIM, PTS), jnp.float32),
        ],
        compiler_params=pltpu.CompilerParams(vmem_limit_bytes=32 * 2**20),
        cost_estimate=pl.CostEstimate(
            flops=2 * 320 * PTS * 256 * 256, bytes_accessed=12 * 2**20, transcendentals=10**7
        ),
    )(meta, r_list, q_list, x_rows, source, *final)


def shifted(block, axis, distance):
    devices = range(lax.axis_size(axis))
    route = [(i - distance, i) for i in devices if i - distance in devices]
    return lax.ppermute(block, axis, route)


def local(
    history,
    positions,
    kappa_old,
    threshold,
    pair_ids,
    reader_counts,
    brick_map,
    strain_disp,
    couple,
):
    points = positions[0].transpose(1, 0, 2)
    own = jnp.concatenate(
        [history[0].reshape(HIST_ROWS, PTS), points.reshape(3 * CL, PTS)], axis=0
    )
    tile = lax.axis_index("tile")
    lists = make_lists(pair_ids[0].T, reader_counts, tile.astype(jnp.int32).reshape(1), points)
    source = lax.all_gather(own, "tile", axis=0, tiled=False)
    brick = brick_map - (tile - 1) * BR_DEV
    damage_here, shares = consume(
        lists, source, (kappa_old[0], threshold[0], strain_disp, brick)
    )
    low, mid, top = shares[:BR_DEV], shares[BR_DEV : 2 * BR_DEV], shares[2 * BR_DEV :]
    force = mid + shifted(top, "tile", 1) + shifted(low, "tile", -1)
    before = shifted(force[-1:], "slab", 1)
    after = shifted(force[:1], "slab", -1)
    padded = jnp.concatenate([before, force, after], axis=0)
    residual_here = force + jnp.dot(
        padded[:-2] + padded[2:],
        couple,
        precision=lax.Precision.HIGHEST,
        preferred_element_type=jnp.float32,
    )
    return (damage_here[None], residual_here[:, None, :])


def solution(mesh):
    placed = (
        P("slab", "tile", None, None),
        P("slab", "tile", None, None),
        P("slab", "tile", None),
        P("slab", "tile", None),
        P("slab", "tile", None),
        P("slab", "tile"),
        P("slab", "tile"),
        P(),
        P(),
    )
    return jax.shard_map(
        local,
        mesh=mesh,
        in_specs=placed,
        out_specs=(P("slab", "tile", None), P("slab", "tile", None)),
        check_vma=False,
    )
```

```python
import functools
import math

import jax
import jax.numpy as jnp
from jax import lax
from jax.experimental import pallas as pl
from jax.experimental.pallas import tpu as pltpu
from jax.sharding import PartitionSpec as P

PTS = 128
COLS = 8
PAIRS = 8
CL = 128
BR_DEV = 32
N_TILE = 16
SHARP = 12.0
SOFTEN = 2.0
SCALE = SHARP * math.log2(math.e)

UNITS = 8
STEP = 2 * UNITS
ROUNDS = N_TILE // 2 + 1
REGION = CL * PAIRS
YDIM = 8
KDIM = 2 * YDIM
HIST_ROWS = CL * COLS
ACC_ROWS = (CL + 1) * 2 * COLS
SMEM = pl.BlockSpec(memory_space=pltpu.SMEM)
VMEM = pl.BlockSpec(memory_space=pltpu.VMEM)


def split2(x):
    hi = x.astype(jnp.bfloat16).astype(jnp.float32)
    return hi, x - hi


def split3(x):
    hi, rest = split2(x)
    return (hi,) + split2(rest)


def reader_rows(here_ref, rows_ref, x_ref):
    here = [here_ref[k].astype(jnp.float32) for k in range(3)]
    twice = [split2((2.0 * SCALE) * h) for h in here]
    norm = split2(-SCALE * (here[0] * here[0] + here[1] * here[1] + here[2] * here[2]))
    one = jnp.ones((CL, PTS), jnp.float32)
    none = jnp.zeros((CL, PTS), jnp.float32)
    rows = [twice[k][0] for k in range(3)] + [one] * 3 + [norm[0], none]
    rows += [twice[k][1] for k in range(3)] + [none] * 3 + [norm[1], none]
    for k, row in enumerate(rows):
        rows_ref[pl.ds(k, CL, stride=KDIM), :] = row

    def turn(g, carry):
        four = [
            rows_ref[pl.ds(pl.multiple_of((g * 4 + m) * KDIM, KDIM), KDIM), :] for m in range(4)
        ]
        turned = jnp.concatenate([f for f in four for _ in range(2)], axis=0).T
        turned = turned.astype(jnp.bfloat16)
        for m in range(4):
            x_ref[g * 4 + m] = turned[:, m * 2 * KDIM : (m + 1) * 2 * KDIM]
        return carry

    lax.fori_loop(0, CL // 4, turn, 0)


def setup_kernel(ids_ref, cnt_ref, tile_ref, here_ref, list_ref, steps_ref, x_ref, cur_ref, rows_ref):
    reader_rows(here_ref, rows_ref, x_ref)
    tile = tile_ref[0]
    for k in range(ROUNDS + 1):
        cur_ref[k] = k * REGION

    def reader(r, carry):
        count = cnt_ref[0, r]
        for p in range(PAIRS):
            q = ids_ref[p, r]
            d = ((q >> 7) - tile) & (N_TILE - 1)
            near = jnp.minimum(d, N_TILE - d)
            k = jnp.where(p < count, near, ROUNDS)
            slot = jnp.where(d == near, CL, 0)
            at = cur_ref[k]
            list_ref[at] = (r << 8) | slot | (q & (CL - 1))
            cur_ref[k] = at + 1
        return carry

    lax.fori_loop(0, CL, reader, 0)
    for k in range(ROUNDS):
        used = cur_ref[k]
        steps = (used - k * REGION + (STEP - 1)) >> 4
        steps_ref[k] = steps

        def pad(at, carry):
            list_ref[at] = (CL << 8) | CL
            return carry

        lax.fori_loop(used, k * REGION + steps * STEP, pad, 0)


def setup(ids, counts, tile, here):
    return pl.pallas_call(
        setup_kernel,
        out_shape=[
            jax.ShapeDtypeStruct(((ROUNDS + 1) * REGION,), jnp.int32),
            jax.ShapeDtypeStruct((ROUNDS,), jnp.int32),
            jax.ShapeDtypeStruct((CL, PTS, 2 * KDIM), jnp.bfloat16),
        ],
        in_specs=[SMEM] * 3 + [VMEM],
        out_specs=[SMEM] * 2 + [VMEM],
        scratch_shapes=[
            pltpu.SMEM((ROUNDS + 1,), jnp.int32),
            pltpu.VMEM((CL * KDIM, PTS), jnp.float32),
        ],
        compiler_params=pltpu.CompilerParams(vmem_limit_bytes=16 * 2**20),
        cost_estimate=pl.CostEstimate(flops=10**6, bytes_accessed=10**7, transcendentals=0),
    )(ids, counts, tile, here)


def prepare(slot, parts, hist_ref, y_ref):
    base = slot * HIST_ROWS
    at = 0
    spots = []
    for part in parts:
        rows = part.shape[0]
        take = min(rows, HIST_ROWS - at)
        if take > 0:
            hist_ref[base + at : base + at + take] = part[:take].astype(jnp.float32)
            at += take
        for k in range(max(take, 0), rows, CL):
            spots.append(part[k : k + CL].astype(jnp.float32))
    norm = spots[0] * spots[0] + spots[1] * spots[1] + spots[2] * spots[2]
    one = jnp.ones((CL, PTS), jnp.float32)
    rows = spots + list(split3(-SCALE * norm)) + [one, 0.0 * one]
    for k, row in enumerate(rows):
        y_ref[pl.ds(base + k, CL, stride=YDIM), :] = row


def pairs(base, steps, list_s, x_ref, hist_ref, y_ref, acc_ref):
    first = lax.broadcasted_iota(jnp.int32, (PTS, 2 * KDIM), 1) < KDIM
    zero_y = jnp.zeros((KDIM, PTS), jnp.float32)
    zero_h = jnp.zeros((COLS, PTS), jnp.float32)
    row = lax.broadcasted_iota(jnp.int32, (2 * COLS, 2 * PTS), 0) >> 3
    side = lax.broadcasted_iota(jnp.int32, (2 * COLS, 2 * PTS), 1) >> 7
    ones = (row == side).astype(jnp.float32).astype(jnp.bfloat16)

    def beside(one, other, zero):
        top = jnp.concatenate([one, zero], axis=1)
        bottom = jnp.concatenate([zero, other], axis=1)
        return jnp.concatenate([top, bottom], axis=0).astype(jnp.bfloat16)

    def eight(ref, k):
        return ref[pl.ds(pl.multiple_of(k * 8, 8), 8), :]

    def step(i, carry):
        entries = [list_s[base + i * STEP + k] for k in range(STEP)]
        readers = [e >> 8 for e in entries]
        sources = [e & (2 * CL - 1) for e in entries]
        units = [(2 * u, 2 * u + 1) for u in range(UNITS)]
        weights = []
        for a, b in units:
            lhs = jnp.where(first, x_ref[readers[a] & (CL - 1)], x_ref[readers[b] & (CL - 1)])
            ys = [eight(y_ref, sources[k]) for k in (a, b)]
            rhs = beside(*[jnp.concatenate([y, y], axis=0) for y in ys], zero_y)
            power = jnp.dot(lhs, rhs, preferred_element_type=jnp.float32)
            weights.append(jnp.exp2(power).astype(jnp.bfloat16))
        outs = []
        for (a, b), weight in zip(units, weights):
            hs = [eight(hist_ref, sources[k]) for k in (a, b)]
            both = jnp.concatenate([beside(*hs, zero_h), ones], axis=0)
            outs.append(
                lax.dot_general(
                    both, weight, (((1,), (1,)), ((), ())), preferred_element_type=jnp.float32
                )
            )
        for unit, out in zip(units, outs):
            for half in range(2):
                at = pl.multiple_of(readers[unit[half]] * (2 * COLS), 2 * COLS)
                acc_ref[pl.ds(at, COLS), :] += out[half * COLS : (half + 1) * COLS]
                acc_ref[pl.ds(at + COLS, COLS), :] += out[(2 + half) * COLS : (3 + half) * COLS]
        return carry

    lax.fori_loop(0, steps, step, 0)


def finish(acc_ref, kappa_ref, threshold_ref, disp_ref, brick_ref, damage_ref, shares_ref):
    inverse = 1.0 / acc_ref[pl.ds(COLS, CL, stride=2 * COLS), :]
    threshold = threshold_ref[...]
    strain = acc_ref[pl.ds(0, CL, stride=2 * COLS), :] * inverse
    kappa = jnp.maximum(jnp.maximum(kappa_ref[...], strain), threshold)
    damage = 1.0 - (threshold / kappa) * jnp.exp(-(kappa - threshold) / SOFTEN)
    damage_ref[...] = damage
    left = 1.0 - damage
    term = jnp.zeros((CL, PTS), jnp.float32)
    for c in range(COLS):
        mean = acc_ref[pl.ds(c, CL, stride=2 * COLS), :] * inverse
        term = term + jnp.dot(
            (left * mean).astype(jnp.bfloat16),
            disp_ref[c * PTS : (c + 1) * PTS, :],
            preferred_element_type=jnp.float32,
        )
    rows = lax.broadcasted_iota(jnp.int32, (3 * BR_DEV, CL), 0)
    onehot = (rows == brick_ref[...]).astype(jnp.float32)
    shares_ref[...] = jnp.dot(
        onehot, term, precision=lax.Precision.HIGHEST, preferred_element_type=jnp.float32
    )


def ring_kernel(round_, sizes, has_acc, final, *refs):
    refs = list(refs)
    take = lambda n: [refs.pop(0) for _ in range(n)]
    steps_s, list_s, x_ref = take(3)
    blocks = [take(n) for n in sizes]
    acc_in = take(1)[0] if has_acc else None
    final_in = take(4) if final else None
    final_out = take(2) if final else None
    acc_ref, hist_ref, y_ref = take(3)
    acc_ref[...] = acc_in[...] if has_acc else jnp.zeros_like(acc_ref)
    for slot, parts in enumerate(blocks):
        prepare(slot if len(blocks) == 2 else 1, parts, hist_ref, y_ref)
    pairs(round_ * REGION, steps_s[round_], list_s, x_ref, hist_ref, y_ref, acc_ref)
    if final:
        finish(acc_ref, *final_in, *final_out)


def consume(prepared, round_, blocks, acc, final=None):
    lists, steps, x_rows = prepared
    args = [steps, lists, x_rows] + [part for parts in blocks for part in parts]
    if acc is not None:
        args.append(acc)
    acc_shape = (ACC_ROWS, PTS)
    scratch = [
        pltpu.VMEM((2 * HIST_ROWS, PTS), jnp.float32),
        pltpu.VMEM((2 * CL * YDIM, PTS), jnp.float32),
    ]
    if final is None:
        out_shape = jax.ShapeDtypeStruct(acc_shape, jnp.float32)
        out_specs = VMEM
    else:
        args += list(final)
        out_shape = [
            jax.ShapeDtypeStruct((CL, PTS), jnp.float32),
            jax.ShapeDtypeStruct((3 * BR_DEV, PTS), jnp.float32),
        ]
        out_specs = [VMEM] * 2
        scratch = [pltpu.VMEM(acc_shape, jnp.float32)] + scratch
    sizes = tuple(len(parts) for parts in blocks)
    return pl.pallas_call(
        functools.partial(ring_kernel, round_, sizes, acc is not None, final is not None),
        out_shape=out_shape,
        in_specs=[SMEM] * 2 + [VMEM] * (len(args) - 2),
        out_specs=out_specs,
        scratch_shapes=scratch,
        compiler_params=pltpu.CompilerParams(vmem_limit_bytes=16 * 2**20),
        cost_estimate=pl.CostEstimate(
            flops=2 * 40 * PTS * 256 * 256, bytes_accessed=8 * 2**20, transcendentals=10**6
        ),
    )(*args)


def hop(block, distance):
    peers = lax.axis_size("tile")
    return lax.ppermute(block, "tile", [(i, (i + distance) % peers) for i in range(peers)])


def shifted(block, axis, distance):
    devices = range(lax.axis_size(axis))
    route = [(i - distance, i) for i in devices if i - distance in devices]
    return lax.ppermute(block, axis, route)


def local(
    history,
    positions,
    kappa_old,
    threshold,
    pair_ids,
    reader_counts,
    brick_map,
    strain_disp,
    couple,
):
    points = positions[0].transpose(1, 0, 2)
    own = jnp.concatenate(
        [history[0].reshape(HIST_ROWS, PTS), points.reshape(3 * CL, PTS)], axis=0
    )
    tile = lax.axis_index("tile")
    half = own.shape[0] // 2
    up, down = hop(own, 1), hop(own, -1)
    prepared = setup(pair_ids[0].T, reader_counts, tile.astype(jnp.int32).reshape(1), points)
    acc = consume(prepared, 0, [[own]], None)
    for s in range(1, N_TILE // 2):
        up, down, acc = lax.optimization_barrier((up, down, acc))
        block = [[up], [down]]
        if s + 1 < N_TILE // 2:
            up, down = hop(up, 1), hop(down, -1)
        else:
            far = [hop(up[:half], 1), hop(down[half:], -1)]
        acc = consume(prepared, s, block, acc)
    brick = brick_map - (tile - 1) * BR_DEV
    damage_here, shares = consume(
        prepared, N_TILE // 2, [far], acc, (kappa_old[0], threshold[0], strain_disp, brick)
    )
    low, mid, top = shares[:BR_DEV], shares[BR_DEV : 2 * BR_DEV], shares[2 * BR_DEV :]
    force = mid + shifted(top, "tile", 1) + shifted(low, "tile", -1)
    before = shifted(force[-1:], "slab", 1)
    after = shifted(force[:1], "slab", -1)
    padded = jnp.concatenate([before, force, after], axis=0)
    residual_here = force + jnp.dot(
        padded[:-2] + padded[2:],
        couple,
        precision=lax.Precision.HIGHEST,
        preferred_element_type=jnp.float32,
    )
    return (damage_here[None], residual_here[:, None, :])


def solution(mesh):
    placed = (
        P("slab", "tile", None, None),
        P("slab", "tile", None, None),
        P("slab", "tile", None),
        P("slab", "tile", None),
        P("slab", "tile", None),
        P("slab", "tile"),
        P("slab", "tile"),
        P(),
        P(),
    )
    return jax.shard_map(
        local,
        mesh=mesh,
        in_specs=placed,
        out_specs=(P("slab", "tile", None), P("slab", "tile", None)),
        check_vma=False,
    )
```

```python
import functools
import math

import jax
import jax.numpy as jnp
from jax import lax
from jax.experimental import pallas as pl
from jax.experimental.pallas import tpu as pltpu
from jax.sharding import PartitionSpec as P

PTS = 128
COLS = 8
PAIRS = 8
CL = 128
BR_DEV = 32
N_TILE = 16
SHARP = 12.0
SOFTEN = 2.0
SCALE = SHARP * math.log2(math.e)

OWN_UNITS = 8
UNITS = 16
LISTED = CL * PAIRS + 2 * UNITS
YDIM = 8
KDIM = 2 * YDIM
HIST_ROWS = CL * COLS
ROWS = HIST_ROWS + 3 * CL
ACC_ROWS = (CL + 1) * 2 * COLS
SMEM = pl.BlockSpec(memory_space=pltpu.SMEM)
VMEM = pl.BlockSpec(memory_space=pltpu.VMEM)
ANY = pl.BlockSpec(memory_space=pl.ANY)


def split2(x):
    hi = x.astype(jnp.bfloat16).astype(jnp.float32)
    return hi, x - hi


def split3(x):
    hi, rest = split2(x)
    return (hi,) + split2(rest)


def reader_rows(here_ref, rows_ref, x_ref):
    here = [here_ref[k].astype(jnp.float32) for k in range(3)]
    twice = [split2((2.0 * SCALE) * h) for h in here]
    norm = split2(-SCALE * (here[0] * here[0] + here[1] * here[1] + here[2] * here[2]))
    one = jnp.ones((CL, PTS), jnp.float32)
    none = jnp.zeros((CL, PTS), jnp.float32)
    rows = [twice[k][0] for k in range(3)] + [one] * 3 + [norm[0], none]
    rows += [twice[k][1] for k in range(3)] + [none] * 3 + [norm[1], none]
    for k, row in enumerate(rows):
        rows_ref[pl.ds(k, CL, stride=KDIM), :] = row

    def turn(g, carry):
        four = [
            rows_ref[pl.ds(pl.multiple_of((g * 4 + m) * KDIM, KDIM), KDIM), :] for m in range(4)
        ]
        turned = jnp.concatenate([f for f in four for _ in range(2)], axis=0).T
        turned = turned.astype(jnp.bfloat16)
        for m in range(4):
            x_ref[g * 4 + m] = turned[:, m * 2 * KDIM : (m + 1) * 2 * KDIM]
        return carry

    lax.fori_loop(0, CL // 4, turn, 0)


def list_pairs(ids_ref, cnt_ref, tile, list_ref, steps_ref, cur_ref):
    for k in range(3):
        cur_ref[k] = k * LISTED

    def reader(r, carry):
        count = cnt_ref[0, r]
        for p in range(PAIRS):
            q = ids_ref[p, r]
            far = jnp.where((q >> 7) == tile, 0, 1)
            k = jnp.where(p < count, far, 2)
            at = cur_ref[k]
            list_ref[at] = (r << 11) | q
            cur_ref[k] = at + 1
        return carry

    lax.fori_loop(0, CL, reader, 0)
    for k, units in ((0, OWN_UNITS), (1, UNITS)):
        used = cur_ref[k] - k * LISTED
        steps = lax.div(used + (2 * units - 1), 2 * units)
        steps_ref[k] = steps

        def pad(at, carry):
            list_ref[at] = CL << 11
            return carry

        lax.fori_loop(k * LISTED + used, k * LISTED + steps * (2 * units), pad, 0)


def source_rows(block, spots, y_ref):
    norm = spots[0] * spots[0] + spots[1] * spots[1] + spots[2] * spots[2]
    one = jnp.ones((CL, PTS), jnp.float32)
    rows = spots + list(split3(-SCALE * norm)) + [one, 0.0 * one]
    for k, row in enumerate(rows):
        y_ref[pl.ds(block * (CL * YDIM) + k, CL, stride=YDIM), :] = row


def pairs(units, base, steps, mask, row_of, list_s, x_ref, hist_ref, y_ref, acc_ref):
    first = lax.broadcasted_iota(jnp.int32, (PTS, 2 * KDIM), 1) < KDIM
    zero_y = jnp.zeros((KDIM, PTS), jnp.float32)
    zero_h = jnp.zeros((COLS, PTS), jnp.float32)
    row = lax.broadcasted_iota(jnp.int32, (2 * COLS, 2 * PTS), 0) >> 3
    side = lax.broadcasted_iota(jnp.int32, (2 * COLS, 2 * PTS), 1) >> 7
    ones = (row == side).astype(jnp.float32).astype(jnp.bfloat16)

    def beside(one, other, zero):
        top = jnp.concatenate([one, zero], axis=1)
        bottom = jnp.concatenate([zero, other], axis=1)
        return jnp.concatenate([top, bottom], axis=0).astype(jnp.bfloat16)

    def source_points(q):
        y = y_ref[pl.ds(pl.multiple_of(q * YDIM, YDIM), YDIM), :]
        return jnp.concatenate([y, y], axis=0)

    def source_hist(q):
        at = pl.multiple_of(row_of(q), 2 * COLS)
        two = hist_ref[pl.ds(at, 2 * COLS), :].astype(jnp.float32)
        return jnp.where((q & 1) == 1, two[COLS:], two[:COLS])

    def step(i, carry):
        entries = [list_s[base + i * (2 * units) + k] for k in range(2 * units)]
        readers = [e >> 11 for e in entries]
        sources = [e & mask for e in entries]
        both = [(2 * u, 2 * u + 1) for u in range(units)]
        weights = []
        for a, b in both:
            lhs = jnp.where(first, x_ref[readers[a] & (CL - 1)], x_ref[readers[b] & (CL - 1)])
            rhs = beside(source_points(sources[a]), source_points(sources[b]), zero_y)
            power = jnp.dot(lhs, rhs, preferred_element_type=jnp.float32)
            weights.append(jnp.exp2(power).astype(jnp.bfloat16))
        outs = []
        for (a, b), weight in zip(both, weights):
            hist = beside(source_hist(sources[a]), source_hist(sources[b]), zero_h)
            outs.append(
                lax.dot_general(
                    jnp.concatenate([hist, ones], axis=0),
                    weight,
                    (((1,), (1,)), ((), ())),
                    preferred_element_type=jnp.float32,
                )
            )
        for unit, out in zip(both, outs):
            for half in range(2):
                at = pl.multiple_of(readers[unit[half]] * (2 * COLS), 2 * COLS)
                acc_ref[pl.ds(at, COLS), :] += out[half * COLS : (half + 1) * COLS]
                acc_ref[pl.ds(at + COLS, COLS), :] += out[(2 + half) * COLS : (3 + half) * COLS]
        return carry

    lax.fori_loop(0, steps, step, 0)


def own_kernel(
    ids_ref,
    cnt_ref,
    tile_ref,
    here_ref,
    hist_ref,
    list_ref,
    steps_ref,
    x_ref,
    acc_ref,
    cur_ref,
    rows_ref,
    y_ref,
):
    reader_rows(here_ref, rows_ref, x_ref)
    list_pairs(ids_ref, cnt_ref, tile_ref[0], list_ref, steps_ref, cur_ref)
    source_rows(0, [here_ref[k].astype(jnp.float32) for k in range(3)], y_ref)
    acc_ref[...] = jnp.zeros_like(acc_ref)
    row_of = lambda q: (q >> 1) * (2 * COLS)
    pairs(
        OWN_UNITS, 0, steps_ref[0], CL - 1, row_of, list_ref, x_ref, hist_ref, y_ref, acc_ref
    )


def own_pairs(ids, counts, tile, here, hist):
    return pl.pallas_call(
        own_kernel,
        out_shape=[
            jax.ShapeDtypeStruct((3 * LISTED,), jnp.int32),
            jax.ShapeDtypeStruct((2,), jnp.int32),
            jax.ShapeDtypeStruct((CL, PTS, 2 * KDIM), jnp.bfloat16),
            jax.ShapeDtypeStruct((ACC_ROWS, PTS), jnp.float32),
        ],
        in_specs=[SMEM] * 3 + [VMEM] * 2,
        out_specs=[SMEM] * 2 + [VMEM] * 2,
        scratch_shapes=[
            pltpu.SMEM((3,), jnp.int32),
            pltpu.VMEM((CL * KDIM, PTS), jnp.float32),
            pltpu.VMEM((CL * YDIM, PTS), jnp.float32),
        ],
        compiler_params=pltpu.CompilerParams(vmem_limit_bytes=16 * 2**20),
        cost_estimate=pl.CostEstimate(
            flops=2 * 80 * PTS * 256 * 256, bytes_accessed=10**7, transcendentals=10**6
        ),
    )(ids, counts, tile, here, hist)


def finish(acc_ref, kappa_ref, threshold_ref, disp_ref, brick_ref, damage_ref, shares_ref):
    inverse = 1.0 / acc_ref[pl.ds(COLS, CL, stride=2 * COLS), :]
    threshold = threshold_ref[...]
    strain = acc_ref[pl.ds(0, CL, stride=2 * COLS), :] * inverse
    kappa = jnp.maximum(jnp.maximum(kappa_ref[...], strain), threshold)
    damage = 1.0 - (threshold / kappa) * jnp.exp(-(kappa - threshold) / SOFTEN)
    damage_ref[...] = damage
    left = 1.0 - damage
    term = jnp.zeros((CL, PTS), jnp.float32)
    for c in range(COLS):
        mean = acc_ref[pl.ds(c, CL, stride=2 * COLS), :] * inverse
        term = term + jnp.dot(
            (left * mean).astype(jnp.bfloat16),
            disp_ref[c * PTS : (c + 1) * PTS, :],
            preferred_element_type=jnp.float32,
        )
    rows = lax.broadcasted_iota(jnp.int32, (3 * BR_DEV, CL), 0)
    onehot = (rows == brick_ref[...]).astype(jnp.float32)
    shares_ref[...] = jnp.dot(
        onehot, term, precision=lax.Precision.HIGHEST, preferred_element_type=jnp.float32
    )


def far_kernel(
    steps_s,
    list_s,
    x_hbm,
    acc_hbm,
    source_hbm,
    kappa_hbm,
    threshold_hbm,
    disp_hbm,
    brick_hbm,
    damage_ref,
    shares_ref,
    x_ref,
    acc_ref,
    source_ref,
    kappa_ref,
    threshold_ref,
    disp_ref,
    brick_ref,
    y_ref,
    sems,
):
    def block_copy(d):
        rows = pl.ds(pl.multiple_of(d * ROWS, ROWS), ROWS)
        return pltpu.make_async_copy(source_hbm.at[d], source_ref.at[rows], sems.at[d])

    others = [
        pltpu.make_async_copy(src, dst, sems.at[N_TILE + k])
        for k, (src, dst) in enumerate(
            (
                (x_hbm, x_ref),
                (acc_hbm, acc_ref),
                (kappa_hbm, kappa_ref),
                (threshold_hbm, threshold_ref),
                (disp_hbm, disp_ref),
                (brick_hbm, brick_ref),
            )
        )
    ]
    for d in range(N_TILE):
        block_copy(d).start()
    for copy in others:
        copy.start()

    def block(d, carry):
        block_copy(d).wait()
        spots = []
        for k in range(3):
            at = pl.multiple_of(d * ROWS + (HIST_ROWS + k * CL), CL)
            spots.append(source_ref[pl.ds(at, CL), :].astype(jnp.float32))
        source_rows(d, spots, y_ref)
        return carry

    lax.fori_loop(0, N_TILE, block, 0)
    for copy in others:
        copy.wait()
    row_of = lambda q: (q >> 7) * ROWS + ((q & (CL - 1)) >> 1) * (2 * COLS)
    pairs(
        UNITS,
        LISTED,
        steps_s[1],
        N_TILE * CL - 1,
        row_of,
        list_s,
        x_ref,
        source_ref,
        y_ref,
        acc_ref,
    )
    finish(acc_ref, kappa_ref, threshold_ref, disp_ref, brick_ref, damage_ref, shares_ref)


def far_pairs(prepared, source, final):
    lists, steps, x_rows, acc = prepared
    held = [x_rows, acc, source.reshape(N_TILE * ROWS, PTS)] + list(final)
    return pl.pallas_call(
        far_kernel,
        out_shape=[
            jax.ShapeDtypeStruct((CL, PTS), jnp.float32),
            jax.ShapeDtypeStruct((3 * BR_DEV, PTS), jnp.float32),
        ],
        in_specs=[SMEM] * 2 + [ANY] * 7,
        out_specs=[VMEM] * 2,
        scratch_shapes=[pltpu.VMEM(h.shape, h.dtype) for h in held]
        + [
            pltpu.VMEM((N_TILE * CL * YDIM, PTS), jnp.float32),
            pltpu.SemaphoreType.DMA((N_TILE + 6,)),
        ],
        compiler_params=pltpu.CompilerParams(vmem_limit_bytes=60 * 2**20),
        cost_estimate=pl.CostEstimate(
            flops=2 * 320 * PTS * 256 * 256, bytes_accessed=12 * 2**20, transcendentals=10**7
        ),
    )(steps, lists, x_rows, acc, source, *final)


def shifted(block, axis, distance):
    devices = range(lax.axis_size(axis))
    route = [(i - distance, i) for i in devices if i - distance in devices]
    return lax.ppermute(block, axis, route)


def local(
    history,
    positions,
    kappa_old,
    threshold,
    pair_ids,
    reader_counts,
    brick_map,
    strain_disp,
    couple,
):
    points = positions[0].transpose(1, 0, 2)
    own = jnp.concatenate(
        [history[0].reshape(HIST_ROWS, PTS), points.reshape(3 * CL, PTS)], axis=0
    )
    tile = lax.axis_index("tile")
    source = lax.all_gather(own, "tile", axis=0, tiled=False)
    prepared = own_pairs(
        pair_ids[0].T,
        reader_counts,
        tile.astype(jnp.int32).reshape(1),
        points,
        history[0].reshape(HIST_ROWS, PTS),
    )
    brick = brick_map - (tile - 1) * BR_DEV
    damage_here, shares = far_pairs(
        prepared, source, (kappa_old[0], threshold[0], strain_disp, brick)
    )
    low, mid, top = shares[:BR_DEV], shares[BR_DEV : 2 * BR_DEV], shares[2 * BR_DEV :]
    force = mid + shifted(top, "tile", 1) + shifted(low, "tile", -1)
    before = shifted(force[-1:], "slab", 1)
    after = shifted(force[:1], "slab", -1)
    padded = jnp.concatenate([before, force, after], axis=0)
    residual_here = force + jnp.dot(
        padded[:-2] + padded[2:],
        couple,
        precision=lax.Precision.HIGHEST,
        preferred_element_type=jnp.float32,
    )
    return (damage_here[None], residual_here[:, None, :])


def solution(mesh):
    placed = (
        P("slab", "tile", None, None),
        P("slab", "tile", None, None),
        P("slab", "tile", None),
        P("slab", "tile", None),
        P("slab", "tile", None),
        P("slab", "tile"),
        P("slab", "tile"),
        P(),
        P(),
    )
    return jax.shard_map(
        local,
        mesh=mesh,
        in_specs=placed,
        out_specs=(P("slab", "tile", None), P("slab", "tile", None)),
        check_vma=False,
    )
```

```python
import functools
import math

import jax
import jax.numpy as jnp
from jax import lax
from jax.experimental import pallas as pl
from jax.experimental.pallas import tpu as pltpu
from jax.sharding import PartitionSpec as P

PTS = 128
COLS = 8
PAIRS = 8
CL = 128
BR_DEV = 32
N_TILE = 16
SHARP = 12.0
SOFTEN = 2.0
SCALE = SHARP * math.log2(math.e)

UNITS = 16
STEP = 2 * UNITS
ROUNDS = N_TILE // 2 + 1
REGION = CL * PAIRS
KEY_SHIFT = 20
YDIM = 8
KDIM = 2 * YDIM
HIST_ROWS = CL * COLS
ACC_ROWS = (CL + 1) * 2 * COLS
SMEM = pl.BlockSpec(memory_space=pltpu.SMEM)
VMEM = pl.BlockSpec(memory_space=pltpu.VMEM)


def split2(x):
    hi = x.astype(jnp.bfloat16).astype(jnp.float32)
    return hi, x - hi


def split3(x):
    hi, rest = split2(x)
    return (hi,) + split2(rest)


def reader_rows(here_ref, rows_ref, x_ref):
    here = [here_ref[k].astype(jnp.float32) for k in range(3)]
    twice = [split2((2.0 * SCALE) * h) for h in here]
    norm = split2(-SCALE * (here[0] * here[0] + here[1] * here[1] + here[2] * here[2]))
    one = jnp.ones((CL, PTS), jnp.float32)
    none = jnp.zeros((CL, PTS), jnp.float32)
    rows = [twice[k][0] for k in range(3)] + [one] * 3 + [norm[0], none]
    rows += [twice[k][1] for k in range(3)] + [none] * 3 + [norm[1], none]
    for k, row in enumerate(rows):
        rows_ref[pl.ds(k, CL, stride=KDIM), :] = row

    def turn(i, carry):
        for u in range(4):
            g = i * 4 + u
            four = [
                rows_ref[pl.ds(pl.multiple_of((g * 4 + m) * KDIM, KDIM), KDIM), :]
                for m in range(4)
            ]
            turned = jnp.concatenate([f for f in four for _ in range(2)], axis=0).T
            turned = turned.astype(jnp.bfloat16)
            for m in range(4):
                x_ref[g * 4 + m] = turned[:, m * 2 * KDIM : (m + 1) * 2 * KDIM]
        return carry

    lax.fori_loop(0, CL // 16, turn, 0)


def setup_kernel(key_ref, here_ref, list_ref, steps_ref, x_ref, cur_ref, rows_ref):
    reader_rows(here_ref, rows_ref, x_ref)
    for k in range(ROUNDS):
        cur_ref[k] = k * REGION

    def reader(r, carry):
        for p in range(PAIRS):
            key = key_ref[p, r]
            k = key >> KEY_SHIFT

            @pl.when(k < ROUNDS)
            def _():
                at = cur_ref[k]
                list_ref[at] = key & ((1 << KEY_SHIFT) - 1)
                cur_ref[k] = at + 1

        return carry

    lax.fori_loop(0, CL, reader, 0)
    for k in range(ROUNDS):
        used = cur_ref[k] - k * REGION
        steps = (used + (STEP - 1)) >> 5
        steps_ref[k] = steps

        def pad(at, carry):
            list_ref[at] = (CL << 9) | CL
            return carry

        lax.fori_loop(k * REGION + used, k * REGION + steps * STEP, pad, 0)


def setup(keys, here):
    return pl.pallas_call(
        setup_kernel,
        out_shape=[
            jax.ShapeDtypeStruct((ROUNDS * REGION,), jnp.int32),
            jax.ShapeDtypeStruct((ROUNDS,), jnp.int32),
            jax.ShapeDtypeStruct((CL, PTS, 2 * KDIM), jnp.bfloat16),
        ],
        in_specs=[SMEM, VMEM],
        out_specs=[SMEM] * 2 + [VMEM],
        scratch_shapes=[
            pltpu.SMEM((ROUNDS,), jnp.int32),
            pltpu.VMEM((CL * KDIM, PTS), jnp.float32),
        ],
        compiler_params=pltpu.CompilerParams(vmem_limit_bytes=16 * 2**20),
        cost_estimate=pl.CostEstimate(flops=10**6, bytes_accessed=10**7, transcendentals=0),
    )(keys, here)


def pair_keys(ids, counts, tile):
    reader = lax.broadcasted_iota(jnp.int32, ids.shape, 1)
    entry = lax.broadcasted_iota(jnp.int32, ids.shape, 0)
    ahead = ((ids >> 7) - tile) & (N_TILE - 1)
    near = jnp.minimum(ahead, N_TILE - ahead)
    own = ahead == 0
    slot = jnp.where(own, 2, jnp.where(ahead == near, 1, 0))
    turn = jnp.where(own, 1 + lax.rem(reader, ROUNDS - 2), near)
    turn = jnp.where(entry < counts, turn, ROUNDS)
    return (turn << KEY_SHIFT) | (reader << 9) | (slot << 7) | (ids & (CL - 1))


def source_rows(block, spots, y_ref):
    norm = spots[0] * spots[0] + spots[1] * spots[1] + spots[2] * spots[2]
    one = jnp.ones((CL, PTS), jnp.float32)
    rows = spots + list(split3(-SCALE * norm)) + [one, 0.0 * one]
    for k, row in enumerate(rows):
        y_ref[pl.ds(block * (CL * YDIM) + k, CL, stride=YDIM), :] = row


def pairs(base, steps, list_s, x_ref, hist_ref, y_ref, acc_ref):
    first = lax.broadcasted_iota(jnp.int32, (PTS, 2 * KDIM), 1) < KDIM
    zero_y = jnp.zeros((KDIM, PTS), jnp.float32)
    zero_h = jnp.zeros((COLS, PTS), jnp.float32)
    row = lax.broadcasted_iota(jnp.int32, (2 * COLS, 2 * PTS), 0) >> 3
    side = lax.broadcasted_iota(jnp.int32, (2 * COLS, 2 * PTS), 1) >> 7
    ones = (row == side).astype(jnp.float32).astype(jnp.bfloat16)

    def beside(one, other, zero):
        top = jnp.concatenate([one, zero], axis=1)
        bottom = jnp.concatenate([zero, other], axis=1)
        return jnp.concatenate([top, bottom], axis=0).astype(jnp.bfloat16)

    def source_points(q):
        y = y_ref[pl.ds(pl.multiple_of(q * YDIM, YDIM), YDIM), :]
        return jnp.concatenate([y, y], axis=0)

    def source_hist(q):
        at = pl.multiple_of((q >> 1) * (2 * COLS), 2 * COLS)
        two = hist_ref[pl.ds(at, 2 * COLS), :].astype(jnp.float32)
        return jnp.where((q & 1) == 1, two[COLS:], two[:COLS])

    def step(i, carry):
        entries = [list_s[base + i * STEP + k] for k in range(STEP)]
        readers = [e >> 9 for e in entries]
        sources = [e & (4 * CL - 1) for e in entries]
        both = [(2 * u, 2 * u + 1) for u in range(UNITS)]
        weights = []
        for a, b in both:
            lhs = jnp.where(first, x_ref[readers[a] & (CL - 1)], x_ref[readers[b] & (CL - 1)])
            rhs = beside(source_points(sources[a]), source_points(sources[b]), zero_y)
            power = jnp.dot(lhs, rhs, preferred_element_type=jnp.float32)
            weights.append(jnp.exp2(power).astype(jnp.bfloat16))
        outs = []
        for (a, b), weight in zip(both, weights):
            hist = beside(source_hist(sources[a]), source_hist(sources[b]), zero_h)
            outs.append(
                lax.dot_general(
                    jnp.concatenate([hist, ones], axis=0),
                    weight,
                    (((1,), (1,)), ((), ())),
                    preferred_element_type=jnp.float32,
                )
            )
        for unit, out in zip(both, outs):
            for half in range(2):
                at = pl.multiple_of(readers[unit[half]] * (2 * COLS), 2 * COLS)
                acc_ref[pl.ds(at, COLS), :] += out[half * COLS : (half + 1) * COLS]
                acc_ref[pl.ds(at + COLS, COLS), :] += out[(2 + half) * COLS : (3 + half) * COLS]
        return carry

    lax.fori_loop(0, steps, step, 0)


def prepare(slot, parts, hist_ref, y_ref):
    at = 0
    spots = []
    for part in parts:
        rows = part.shape[0]
        take = min(rows, HIST_ROWS - at)
        if take > 0:
            base = slot * HIST_ROWS + at
            hist_ref[base : base + take] = part[:take]
            at += take
        for k in range(max(take, 0), rows, CL):
            spots.append(part[k : k + CL].astype(jnp.float32))
    source_rows(slot, spots, y_ref)


def finish(acc_ref, kappa_ref, threshold_ref, disp_ref, brick_ref, damage_ref, shares_ref):
    inverse = 1.0 / acc_ref[pl.ds(COLS, CL, stride=2 * COLS), :]
    threshold = threshold_ref[...]
    strain = acc_ref[pl.ds(0, CL, stride=2 * COLS), :] * inverse
    kappa = jnp.maximum(jnp.maximum(kappa_ref[...], strain), threshold)
    damage = 1.0 - (threshold / kappa) * jnp.exp(-(kappa - threshold) / SOFTEN)
    damage_ref[...] = damage
    left = 1.0 - damage
    term = jnp.zeros((CL, PTS), jnp.float32)
    for c in range(COLS):
        mean = acc_ref[pl.ds(c, CL, stride=2 * COLS), :] * inverse
        term = term + jnp.dot(
            (left * mean).astype(jnp.bfloat16),
            disp_ref[c * PTS : (c + 1) * PTS, :],
            preferred_element_type=jnp.float32,
        )
    rows = lax.broadcasted_iota(jnp.int32, (3 * BR_DEV, CL), 0)
    onehot = (rows == brick_ref[...]).astype(jnp.float32)
    shares_ref[...] = jnp.dot(
        onehot, term, precision=lax.Precision.HIGHEST, preferred_element_type=jnp.float32
    )


def ring_kernel(turn, shape, has_acc, final, *refs):
    refs = list(refs)
    take = lambda n: [refs.pop(0) for _ in range(n)]
    steps_s, list_s, x_ref = take(3)
    blocks = [(slot, take(n)) for slot, n in shape]
    acc_in = take(1)[0] if has_acc else None
    final_in = take(4) if final else None
    final_out = take(2) if final else None
    acc_ref, hist_ref, y_ref = take(3)
    acc_ref[...] = acc_in[...] if has_acc else jnp.zeros_like(acc_ref)
    for slot, parts in blocks:
        prepare(slot, parts, hist_ref, y_ref)
    pairs(turn * REGION, steps_s[turn], list_s, x_ref, hist_ref, y_ref, acc_ref)
    if final:
        finish(acc_ref, *final_in, *final_out)


def consume(prepared, turn, blocks, acc, final=None):
    lists, steps, x_rows = prepared
    args = [steps, lists, x_rows] + [part for _, parts in blocks for part in parts]
    if acc is not None:
        args.append(acc)
    acc_shape = (ACC_ROWS, PTS)
    scratch = [
        pltpu.VMEM((3 * HIST_ROWS, PTS), jnp.bfloat16),
        pltpu.VMEM((3 * CL * YDIM, PTS), jnp.float32),
    ]
    if final is None:
        out_shape = jax.ShapeDtypeStruct(acc_shape, jnp.float32)
        out_specs = VMEM
    else:
        args += list(final)
        out_shape = [
            jax.ShapeDtypeStruct((CL, PTS), jnp.float32),
            jax.ShapeDtypeStruct((3 * BR_DEV, PTS), jnp.float32),
        ]
        out_specs = [VMEM] * 2
        scratch = [pltpu.VMEM(acc_shape, jnp.float32)] + scratch
    shape = tuple((slot, len(parts)) for slot, parts in blocks)
    return pl.pallas_call(
        functools.partial(ring_kernel, turn, shape, acc is not None, final is not None),
        out_shape=out_shape,
        in_specs=[SMEM] * 2 + [VMEM] * (len(args) - 2),
        out_specs=out_specs,
        scratch_shapes=scratch,
        compiler_params=pltpu.CompilerParams(vmem_limit_bytes=16 * 2**20),
        cost_estimate=pl.CostEstimate(
            flops=2 * 40 * PTS * 256 * 256, bytes_accessed=8 * 2**20, transcendentals=10**6
        ),
    )(*args)


def hop(block, distance):
    peers = lax.axis_size("tile")
    return lax.ppermute(block, "tile", [(i, (i + distance) % peers) for i in range(peers)])


def shifted(block, axis, distance):
    devices = range(lax.axis_size(axis))
    route = [(i - distance, i) for i in devices if i - distance in devices]
    return lax.ppermute(block, axis, route)


def local(
    history,
    positions,
    kappa_old,
    threshold,
    pair_ids,
    reader_counts,
    brick_map,
    strain_disp,
    couple,
):
    points = positions[0].transpose(1, 0, 2)
    own = jnp.concatenate(
        [history[0].reshape(HIST_ROWS, PTS), points.reshape(3 * CL, PTS)], axis=0
    )
    tile = lax.axis_index("tile")
    half = own.shape[0] // 2
    last = N_TILE // 2 - 1
    up, down = hop(own, 1), hop(own, -1)
    keys = pair_keys(pair_ids[0].T, reader_counts, tile)
    prepared = setup(keys, points)
    acc = None
    for s in range(1, last + 1):
        block = [(0, [up]), (1, [down]), (2, [own])]
        if acc is None:
            up, prepared = lax.optimization_barrier((up, prepared))
        else:
            up, acc = lax.optimization_barrier((up, acc))
        if s < last:
            up, down = hop(up, 1), hop(down, -1)
        else:
            far = [hop(up[:half], 1), hop(down[half:], -1)]
        acc = consume(prepared, s, block, acc)
    brick = brick_map - (tile - 1) * BR_DEV
    damage_here, shares = consume(
        prepared, last + 1, [(1, far)], acc, (kappa_old[0], threshold[0], strain_disp, brick)
    )
    low, mid, top = shares[:BR_DEV], shares[BR_DEV : 2 * BR_DEV], shares[2 * BR_DEV :]
    force = mid + shifted(top, "tile", 1) + shifted(low, "tile", -1)
    before = shifted(force[-1:], "slab", 1)
    after = shifted(force[:1], "slab", -1)
    padded = jnp.concatenate([before, force, after], axis=0)
    residual_here = force + jnp.dot(
        padded[:-2] + padded[2:],
        couple,
        precision=lax.Precision.HIGHEST,
        preferred_element_type=jnp.float32,
    )
    return (damage_here[None], residual_here[:, None, :])


def solution(mesh):
    placed = (
        P("slab", "tile", None, None),
        P("slab", "tile", None, None),
        P("slab", "tile", None),
        P("slab", "tile", None),
        P("slab", "tile", None),
        P("slab", "tile"),
        P("slab", "tile"),
        P(),
        P(),
    )
    return jax.shard_map(
        local,
        mesh=mesh,
        in_specs=placed,
        out_specs=(P("slab", "tile", None), P("slab", "tile", None)),
        check_vma=False,
    )
```

```python
import functools
import math

import jax
import jax.numpy as jnp
from jax import lax
from jax.experimental import pallas as pl
from jax.experimental.pallas import tpu as pltpu
from jax.sharding import PartitionSpec as P

PTS = 128
COLS = 8
PAIRS = 8
CL = 128
BR_DEV = 32
N_TILE = 16
SHARP = 12.0
SOFTEN = 2.0
SCALE = SHARP * math.log2(math.e)

UNITS = 16
STEP = 2 * UNITS
ROUNDS = N_TILE // 2 + 1
REGION = CL * PAIRS
KEY_SHIFT = 20
YDIM = 8
KDIM = 2 * YDIM
HIST_ROWS = CL * COLS
ACC_ROWS = (CL + 1) * 2 * COLS
SMEM = pl.BlockSpec(memory_space=pltpu.SMEM)
VMEM = pl.BlockSpec(memory_space=pltpu.VMEM)


def split2(x):
    hi = x.astype(jnp.bfloat16).astype(jnp.float32)
    return hi, x - hi


def split3(x):
    hi, rest = split2(x)
    return (hi,) + split2(rest)


def reader_rows(here_ref, rows_ref):
    here = [here_ref[k].astype(jnp.float32) for k in range(3)]
    twice = [split2((2.0 * SCALE) * h) for h in here]
    norm = split2(-SCALE * (here[0] * here[0] + here[1] * here[1] + here[2] * here[2]))
    one = jnp.ones((CL, PTS), jnp.float32)
    none = jnp.zeros((CL, PTS), jnp.float32)
    rows = [twice[k][0] for k in range(3)] + [one] * 3 + [norm[0], none]
    rows += [twice[k][1] for k in range(3)] + [none] * 3 + [norm[1], none]
    for k, row in enumerate(rows):
        rows_ref[pl.ds(k, CL, stride=KDIM), :] = row


def turn_rows(g, rows_ref, x_ref):
    four = [rows_ref[pl.ds(pl.multiple_of((g * 4 + m) * KDIM, KDIM), KDIM), :] for m in range(4)]
    turned = jnp.concatenate([f for f in four for _ in range(2)], axis=0).T
    turned = turned.astype(jnp.bfloat16)
    for m in range(4):
        x_ref[g * 4 + m] = turned[:, m * 2 * KDIM : (m + 1) * 2 * KDIM]


def setup_kernel(key_ref, here_ref, list_ref, steps_ref, x_ref, cur_ref, rows_ref):
    reader_rows(here_ref, rows_ref)
    for k in range(ROUNDS):
        cur_ref[k] = k * REGION

    def sixteen(i, carry):
        for u in range(4):
            turn_rows(i * 4 + u, rows_ref, x_ref)
        for u in range(16):
            for p in range(PAIRS):
                key = key_ref[p, i * 16 + u]
                k = key >> KEY_SHIFT
                at = cur_ref[k]
                list_ref[at] = key & ((1 << KEY_SHIFT) - 1)
                cur_ref[k] = at + 1
        return carry

    lax.fori_loop(0, CL // 16, sixteen, 0)
    for k in range(1, ROUNDS):
        used = cur_ref[k] - k * REGION
        steps = (used + (STEP - 1)) >> 5
        steps_ref[k] = steps

        def pad(at, carry):
            list_ref[at] = (CL << 9) | CL
            return carry

        lax.fori_loop(k * REGION + used, k * REGION + steps * STEP, pad, 0)


def setup(keys, here):
    return pl.pallas_call(
        setup_kernel,
        out_shape=[
            jax.ShapeDtypeStruct((ROUNDS * REGION,), jnp.int32),
            jax.ShapeDtypeStruct((ROUNDS,), jnp.int32),
            jax.ShapeDtypeStruct((CL, PTS, 2 * KDIM), jnp.bfloat16),
        ],
        in_specs=[SMEM, VMEM],
        out_specs=[SMEM] * 2 + [VMEM],
        scratch_shapes=[
            pltpu.SMEM((ROUNDS,), jnp.int32),
            pltpu.VMEM((CL * KDIM, PTS), jnp.float32),
        ],
        compiler_params=pltpu.CompilerParams(vmem_limit_bytes=16 * 2**20),
        cost_estimate=pl.CostEstimate(flops=10**6, bytes_accessed=10**7, transcendentals=0),
    )(keys, here)


def pair_keys(ids, counts, tile):
    reader = lax.broadcasted_iota(jnp.int32, ids.shape, 1)
    entry = lax.broadcasted_iota(jnp.int32, ids.shape, 0)
    ahead = ((ids >> 7) - tile) & (N_TILE - 1)
    near = jnp.minimum(ahead, N_TILE - ahead)
    own = ahead == 0
    slot = jnp.where(own, 2, jnp.where(ahead == near, 1, 0))
    turn = jnp.where(own, 1 + lax.rem(reader, ROUNDS - 2), near)
    turn = jnp.where(entry < counts, turn, 0)
    return (turn << KEY_SHIFT) | (reader << 9) | (slot << 7) | (ids & (CL - 1))


def source_rows(block, spots, y_ref):
    norm = spots[0] * spots[0] + spots[1] * spots[1] + spots[2] * spots[2]
    one = jnp.ones((CL, PTS), jnp.float32)
    rows = spots + list(split3(-SCALE * norm)) + [one, 0.0 * one]
    for k, row in enumerate(rows):
        y_ref[pl.ds(block * (CL * YDIM) + k, CL, stride=YDIM), :] = row


def pairs(base, steps, list_s, x_ref, hist_ref, y_ref, acc_ref):
    first = lax.broadcasted_iota(jnp.int32, (PTS, 2 * KDIM), 1) < KDIM
    zero_y = jnp.zeros((KDIM, PTS), jnp.float32)
    zero_h = jnp.zeros((COLS, PTS), jnp.float32)
    row = lax.broadcasted_iota(jnp.int32, (2 * COLS, 2 * PTS), 0) >> 3
    side = lax.broadcasted_iota(jnp.int32, (2 * COLS, 2 * PTS), 1) >> 7
    ones = (row == side).astype(jnp.float32).astype(jnp.bfloat16)

    def beside(one, other, zero):
        top = jnp.concatenate([one, zero], axis=1)
        bottom = jnp.concatenate([zero, other], axis=1)
        return jnp.concatenate([top, bottom], axis=0).astype(jnp.bfloat16)

    def source_points(q):
        y = y_ref[pl.ds(pl.multiple_of(q * YDIM, YDIM), YDIM), :]
        return jnp.concatenate([y, y], axis=0)

    def source_hist(q):
        at = pl.multiple_of((q >> 1) * (2 * COLS), 2 * COLS)
        two = hist_ref[pl.ds(at, 2 * COLS), :].astype(jnp.float32)
        return jnp.where((q & 1) == 1, two[COLS:], two[:COLS])

    def step(i, carry):
        entries = [list_s[base + i * STEP + k] for k in range(STEP)]
        readers = [e >> 9 for e in entries]
        sources = [e & (4 * CL - 1) for e in entries]
        both = [(2 * u, 2 * u + 1) for u in range(UNITS)]
        weights = []
        for a, b in both:
            lhs = jnp.where(first, x_ref[readers[a] & (CL - 1)], x_ref[readers[b] & (CL - 1)])
            rhs = beside(source_points(sources[a]), source_points(sources[b]), zero_y)
            power = jnp.dot(lhs, rhs, preferred_element_type=jnp.float32)
            weights.append(jnp.exp2(power).astype(jnp.bfloat16))
        outs = []
        for (a, b), weight in zip(both, weights):
            hist = beside(source_hist(sources[a]), source_hist(sources[b]), zero_h)
            outs.append(
                lax.dot_general(
                    jnp.concatenate([hist, ones], axis=0),
                    weight,
                    (((1,), (1,)), ((), ())),
                    preferred_element_type=jnp.float32,
                )
            )
        for unit, out in zip(both, outs):
            for half in range(2):
                at = pl.multiple_of(readers[unit[half]] * (2 * COLS), 2 * COLS)
                acc_ref[pl.ds(at, COLS), :] += out[half * COLS : (half + 1) * COLS]
                acc_ref[pl.ds(at + COLS, COLS), :] += out[(2 + half) * COLS : (3 + half) * COLS]
        return carry

    lax.fori_loop(0, steps, step, 0)


def prepare(slot, parts, hist_ref, y_ref):
    at = 0
    spots = []
    for part in parts:
        rows = part.shape[0]
        take = min(rows, HIST_ROWS - at)
        if take > 0:
            base = slot * HIST_ROWS + at
            hist_ref[base : base + take] = part[:take]
            at += take
        for k in range(max(take, 0), rows, CL):
            spots.append(part[k : k + CL].astype(jnp.float32))
    source_rows(slot, spots, y_ref)


def finish(acc_ref, kappa_ref, threshold_ref, disp_ref, brick_ref, damage_ref, shares_ref):
    inverse = 1.0 / acc_ref[pl.ds(COLS, CL, stride=2 * COLS), :]
    threshold = threshold_ref[...]
    strain = acc_ref[pl.ds(0, CL, stride=2 * COLS), :] * inverse
    kappa = jnp.maximum(jnp.maximum(kappa_ref[...], strain), threshold)
    damage = 1.0 - (threshold / kappa) * jnp.exp(-(kappa - threshold) / SOFTEN)
    damage_ref[...] = damage
    left = 1.0 - damage
    term = jnp.zeros((CL, PTS), jnp.float32)
    for c in range(COLS):
        mean = acc_ref[pl.ds(c, CL, stride=2 * COLS), :] * inverse
        term = term + jnp.dot(
            (left * mean).astype(jnp.bfloat16),
            disp_ref[c * PTS : (c + 1) * PTS, :],
            preferred_element_type=jnp.float32,
        )
    rows = lax.broadcasted_iota(jnp.int32, (3 * BR_DEV, CL), 0)
    onehot = (rows == brick_ref[...]).astype(jnp.float32)
    shares_ref[...] = jnp.dot(
        onehot, term, precision=lax.Precision.HIGHEST, preferred_element_type=jnp.float32
    )


def ring_kernel(turn, shape, has_acc, final, *refs):
    refs = list(refs)
    take = lambda n: [refs.pop(0) for _ in range(n)]
    steps_s, list_s, x_ref = take(3)
    blocks = [(slot, take(n)) for slot, n in shape]
    acc_in = take(1)[0] if has_acc else None
    final_in = take(4) if final else None
    final_out = take(2) if final else None
    acc_ref, hist_ref, y_ref = take(3)
    acc_ref[...] = acc_in[...] if has_acc else jnp.zeros_like(acc_ref)
    for slot, parts in blocks:
        prepare(slot, parts, hist_ref, y_ref)
    pairs(turn * REGION, steps_s[turn], list_s, x_ref, hist_ref, y_ref, acc_ref)
    if final:
        finish(acc_ref, *final_in, *final_out)


def consume(prepared, turn, blocks, acc, final=None):
    lists, steps, x_rows = prepared
    args = [steps, lists, x_rows] + [part for _, parts in blocks for part in parts]
    if acc is not None:
        args.append(acc)
    acc_shape = (ACC_ROWS, PTS)
    scratch = [
        pltpu.VMEM((3 * HIST_ROWS, PTS), jnp.bfloat16),
        pltpu.VMEM((3 * CL * YDIM, PTS), jnp.float32),
    ]
    if final is None:
        out_shape = jax.ShapeDtypeStruct(acc_shape, jnp.float32)
        out_specs = VMEM
    else:
        args += list(final)
        out_shape = [
            jax.ShapeDtypeStruct((CL, PTS), jnp.float32),
            jax.ShapeDtypeStruct((3 * BR_DEV, PTS), jnp.float32),
        ]
        out_specs = [VMEM] * 2
        scratch = [pltpu.VMEM(acc_shape, jnp.float32)] + scratch
    shape = tuple((slot, len(parts)) for slot, parts in blocks)
    return pl.pallas_call(
        functools.partial(ring_kernel, turn, shape, acc is not None, final is not None),
        out_shape=out_shape,
        in_specs=[SMEM] * 2 + [VMEM] * (len(args) - 2),
        out_specs=out_specs,
        scratch_shapes=scratch,
        compiler_params=pltpu.CompilerParams(vmem_limit_bytes=16 * 2**20),
        cost_estimate=pl.CostEstimate(
            flops=2 * 40 * PTS * 256 * 256, bytes_accessed=8 * 2**20, transcendentals=10**6
        ),
    )(*args)


def hop(block, distance):
    peers = lax.axis_size("tile")
    return lax.ppermute(block, "tile", [(i, (i + distance) % peers) for i in range(peers)])


def shifted(block, axis, distance):
    devices = range(lax.axis_size(axis))
    route = [(i - distance, i) for i in devices if i - distance in devices]
    return lax.ppermute(block, axis, route)


def local(
    history,
    positions,
    kappa_old,
    threshold,
    pair_ids,
    reader_counts,
    brick_map,
    strain_disp,
    couple,
):
    points = positions[0].transpose(1, 0, 2)
    own = jnp.concatenate(
        [history[0].reshape(HIST_ROWS, PTS), points.reshape(3 * CL, PTS)], axis=0
    )
    tile = lax.axis_index("tile")
    last = N_TILE // 2 - 1
    up, down = hop(own, 1), hop(own, -1)
    keys = pair_keys(pair_ids[0].T, reader_counts, tile)
    prepared = setup(keys, points)
    acc = None
    for s in range(1, last + 1):
        block = [(0, [up]), (1, [down]), (2, [own])]
        if acc is None:
            up, prepared = lax.optimization_barrier((up, prepared))
        else:
            up, acc = lax.optimization_barrier((up, acc))
        if s < last:
            up, down = hop(up, 1), hop(down, -1)
        else:
            far = hop(up, 1)
        acc = consume(prepared, s, block, acc)
    brick = brick_map - (tile - 1) * BR_DEV
    damage_here, shares = consume(
        prepared, last + 1, [(1, [far])], acc, (kappa_old[0], threshold[0], strain_disp, brick)
    )
    low, mid, top = shares[:BR_DEV], shares[BR_DEV : 2 * BR_DEV], shares[2 * BR_DEV :]
    force = mid + shifted(top, "tile", 1) + shifted(low, "tile", -1)
    before = shifted(force[-1:], "slab", 1)
    after = shifted(force[:1], "slab", -1)
    padded = jnp.concatenate([before, force, after], axis=0)
    residual_here = force + jnp.dot(
        padded[:-2] + padded[2:],
        couple,
        precision=lax.Precision.HIGHEST,
        preferred_element_type=jnp.float32,
    )
    return (damage_here[None], residual_here[:, None, :])


def solution(mesh):
    placed = (
        P("slab", "tile", None, None),
        P("slab", "tile", None, None),
        P("slab", "tile", None),
        P("slab", "tile", None),
        P("slab", "tile", None),
        P("slab", "tile"),
        P("slab", "tile"),
        P(),
        P(),
    )
    return jax.shard_map(
        local,
        mesh=mesh,
        in_specs=placed,
        out_specs=(P("slab", "tile", None), P("slab", "tile", None)),
        check_vma=False,
    )
```

```python
import functools
import math

import jax
import jax.numpy as jnp
from jax import lax
from jax.experimental import pallas as pl
from jax.experimental.pallas import tpu as pltpu
from jax.sharding import PartitionSpec as P

PTS = 128
COLS = 8
PAIRS = 8
CL = 128
BR_DEV = 32
N_TILE = 16
SHARP = 12.0
SOFTEN = 2.0
SCALE = SHARP * math.log2(math.e)

UNITS = 16
STEP = 2 * UNITS
ROUNDS = N_TILE // 2 + 1
REGION = CL * PAIRS
KEY_SHIFT = 20
OWN_ROUNDS = 3
YDIM = 8
KDIM = 2 * YDIM
HIST_ROWS = CL * COLS
ACC_ROWS = (CL + 1) * 2 * COLS
SMEM = pl.BlockSpec(memory_space=pltpu.SMEM)
VMEM = pl.BlockSpec(memory_space=pltpu.VMEM)


def split2(x):
    hi = x.astype(jnp.bfloat16).astype(jnp.float32)
    return hi, x - hi


def split3(x):
    hi, rest = split2(x)
    return (hi,) + split2(rest)


def reader_rows(here_ref, rows_ref):
    here = [
        here_ref[HIST_ROWS + k * CL : HIST_ROWS + (k + 1) * CL].astype(jnp.float32)
        for k in range(3)
    ]
    twice = [split2((2.0 * SCALE) * h) for h in here]
    norm = split2(-SCALE * (here[0] * here[0] + here[1] * here[1] + here[2] * here[2]))
    one = jnp.ones((CL, PTS), jnp.float32)
    none = jnp.zeros((CL, PTS), jnp.float32)
    rows = [twice[k][0] for k in range(3)] + [one] * 3 + [norm[0], none]
    rows += [twice[k][1] for k in range(3)] + [none] * 3 + [norm[1], none]
    for k, row in enumerate(rows):
        rows_ref[pl.ds(k, CL, stride=KDIM), :] = row


def turn_rows(g, rows_ref, x_ref):
    four = [rows_ref[pl.ds(pl.multiple_of((g * 4 + m) * KDIM, KDIM), KDIM), :] for m in range(4)]
    turned = jnp.concatenate([f for f in four for _ in range(2)], axis=0).T
    turned = turned.astype(jnp.bfloat16)
    for m in range(4):
        x_ref[g * 4 + m] = turned[:, m * 2 * KDIM : (m + 1) * 2 * KDIM]


def setup_kernel(key_ref, here_ref, list_ref, steps_ref, x_ref, cur_ref, rows_ref):
    reader_rows(here_ref, rows_ref)
    for k in range(ROUNDS):
        cur_ref[k] = k * REGION

    def sixteen(i, carry):
        for u in range(4):
            turn_rows(i * 4 + u, rows_ref, x_ref)
        for u in range(16):
            for p in range(PAIRS):
                key = key_ref[p, i * 16 + u]
                k = key >> KEY_SHIFT
                at = cur_ref[k]
                list_ref[at] = key & ((1 << KEY_SHIFT) - 1)
                cur_ref[k] = at + 1
        return carry

    lax.fori_loop(0, CL // 16, sixteen, 0)
    for k in range(1, ROUNDS):
        used = cur_ref[k] - k * REGION
        steps = (used + (STEP - 1)) >> 5
        steps_ref[k] = steps

        def pad(at, carry):
            list_ref[at] = (CL << 9) | CL
            return carry

        lax.fori_loop(k * REGION + used, k * REGION + steps * STEP, pad, 0)


def setup(keys, own):
    return pl.pallas_call(
        setup_kernel,
        out_shape=[
            jax.ShapeDtypeStruct((ROUNDS * REGION,), jnp.int32),
            jax.ShapeDtypeStruct((ROUNDS,), jnp.int32),
            jax.ShapeDtypeStruct((CL, PTS, 2 * KDIM), jnp.bfloat16),
        ],
        in_specs=[SMEM, VMEM],
        out_specs=[SMEM] * 2 + [VMEM],
        scratch_shapes=[
            pltpu.SMEM((ROUNDS,), jnp.int32),
            pltpu.VMEM((CL * KDIM, PTS), jnp.float32),
        ],
        compiler_params=pltpu.CompilerParams(vmem_limit_bytes=16 * 2**20),
        cost_estimate=pl.CostEstimate(flops=10**6, bytes_accessed=10**7, transcendentals=0),
    )(keys, own)


def pair_keys(ids, counts, tile):
    reader = lax.broadcasted_iota(jnp.int32, ids.shape, 1)
    entry = lax.broadcasted_iota(jnp.int32, ids.shape, 0)
    ahead = ((ids >> 7) - tile) & (N_TILE - 1)
    near = jnp.minimum(ahead, N_TILE - ahead)
    own = ahead == 0
    slot = jnp.where(own, 2, jnp.where(ahead == near, 1, 0))
    turn = jnp.where(own, 1 + lax.rem(reader, OWN_ROUNDS), near)
    turn = jnp.where(entry < counts, turn, 0)
    return (turn << KEY_SHIFT) | (reader << 9) | (slot << 7) | (ids & (CL - 1))


def source_rows(block, spots, y_ref):
    norm = spots[0] * spots[0] + spots[1] * spots[1] + spots[2] * spots[2]
    one = jnp.ones((CL, PTS), jnp.float32)
    rows = spots + list(split3(-SCALE * norm)) + [one, 0.0 * one]
    for k, row in enumerate(rows):
        y_ref[pl.ds(block * (CL * YDIM) + k, CL, stride=YDIM), :] = row


def pairs(base, steps, list_s, x_ref, hist_ref, y_ref, acc_ref):
    first = lax.broadcasted_iota(jnp.int32, (PTS, 2 * KDIM), 1) < KDIM
    zero_y = jnp.zeros((KDIM, PTS), jnp.float32)
    zero_h = jnp.zeros((COLS, PTS), jnp.float32)
    row = lax.broadcasted_iota(jnp.int32, (2 * COLS, 2 * PTS), 0) >> 3
    side = lax.broadcasted_iota(jnp.int32, (2 * COLS, 2 * PTS), 1) >> 7
    ones = (row == side).astype(jnp.float32).astype(jnp.bfloat16)

    def beside(one, other, zero):
        top = jnp.concatenate([one, zero], axis=1)
        bottom = jnp.concatenate([zero, other], axis=1)
        return jnp.concatenate([top, bottom], axis=0).astype(jnp.bfloat16)

    def source_points(q):
        y = y_ref[pl.ds(pl.multiple_of(q * YDIM, YDIM), YDIM), :]
        return jnp.concatenate([y, y], axis=0)

    def source_hist(q):
        at = pl.multiple_of((q >> 1) * (2 * COLS), 2 * COLS)
        two = hist_ref[pl.ds(at, 2 * COLS), :].astype(jnp.float32)
        return jnp.where((q & 1) == 1, two[COLS:], two[:COLS])

    def step(i, carry):
        entries = [list_s[base + i * STEP + k] for k in range(STEP)]
        readers = [e >> 9 for e in entries]
        sources = [e & (4 * CL - 1) for e in entries]
        both = [(2 * u, 2 * u + 1) for u in range(UNITS)]
        weights = []
        for a, b in both:
            lhs = jnp.where(first, x_ref[readers[a] & (CL - 1)], x_ref[readers[b] & (CL - 1)])
            rhs = beside(source_points(sources[a]), source_points(sources[b]), zero_y)
            power = jnp.dot(lhs, rhs, preferred_element_type=jnp.float32)
            weights.append(jnp.exp2(power).astype(jnp.bfloat16))
        outs = []
        for (a, b), weight in zip(both, weights):
            hist = beside(source_hist(sources[a]), source_hist(sources[b]), zero_h)
            outs.append(
                lax.dot_general(
                    jnp.concatenate([hist, ones], axis=0),
                    weight,
                    (((1,), (1,)), ((), ())),
                    preferred_element_type=jnp.float32,
                )
            )
        for unit, out in zip(both, outs):
            for half in range(2):
                at = pl.multiple_of(readers[unit[half]] * (2 * COLS), 2 * COLS)
                acc_ref[pl.ds(at, COLS), :] += out[half * COLS : (half + 1) * COLS]
                acc_ref[pl.ds(at + COLS, COLS), :] += out[(2 + half) * COLS : (3 + half) * COLS]
        return carry

    lax.fori_loop(0, steps, step, 0)


def prepare(slot, parts, hist_ref, y_ref):
    at = 0
    spots = []
    for part in parts:
        rows = part.shape[0]
        take = min(rows, HIST_ROWS - at)
        if take > 0:
            base = slot * HIST_ROWS + at
            hist_ref[base : base + take] = part[:take]
            at += take
        for k in range(max(take, 0), rows, CL):
            spots.append(part[k : k + CL].astype(jnp.float32))
    source_rows(slot, spots, y_ref)


def finish(acc_ref, kappa_ref, threshold_ref, disp_ref, brick_ref, damage_ref, shares_ref):
    inverse = 1.0 / acc_ref[pl.ds(COLS, CL, stride=2 * COLS), :]
    threshold = threshold_ref[...]
    strain = acc_ref[pl.ds(0, CL, stride=2 * COLS), :] * inverse
    kappa = jnp.maximum(jnp.maximum(kappa_ref[...], strain), threshold)
    damage = 1.0 - (threshold / kappa) * jnp.exp(-(kappa - threshold) / SOFTEN)
    damage_ref[...] = damage
    left = 1.0 - damage
    term = jnp.zeros((CL, PTS), jnp.float32)
    for c in range(COLS):
        mean = acc_ref[pl.ds(c, CL, stride=2 * COLS), :] * inverse
        term = term + jnp.dot(
            (left * mean).astype(jnp.bfloat16),
            disp_ref[c * PTS : (c + 1) * PTS, :],
            preferred_element_type=jnp.float32,
        )
    rows = lax.broadcasted_iota(jnp.int32, (3 * BR_DEV, CL), 0)
    onehot = (rows == brick_ref[...]).astype(jnp.float32)
    shares_ref[...] = jnp.dot(
        onehot, term, precision=lax.Precision.HIGHEST, preferred_element_type=jnp.float32
    )


def ring_kernel(turn, shape, has_acc, final, *refs):
    refs = list(refs)
    take = lambda n: [refs.pop(0) for _ in range(n)]
    steps_s, list_s, x_ref = take(3)
    blocks = [(slot, take(n)) for slot, n in shape]
    acc_in = take(1)[0] if has_acc else None
    final_in = take(4) if final else None
    final_out = take(2) if final else None
    acc_ref, hist_ref, y_ref = take(3)
    acc_ref[...] = acc_in[...] if has_acc else jnp.zeros_like(acc_ref)
    for slot, parts in blocks:
        prepare(slot, parts, hist_ref, y_ref)
    pairs(0 if final else turn * REGION, steps_s[turn], list_s, x_ref, hist_ref, y_ref, acc_ref)
    if final:
        finish(acc_ref, *final_in, *final_out)


def consume(prepared, turn, blocks, acc, final=None):
    lists, steps, x_rows = prepared
    if final is not None:
        lists = lists[turn * REGION : (turn + 1) * REGION]
    args = [steps, lists, x_rows] + [part for _, parts in blocks for part in parts]
    if acc is not None:
        args.append(acc)
    acc_shape = (ACC_ROWS, PTS)
    scratch = [
        pltpu.VMEM((3 * HIST_ROWS, PTS), jnp.bfloat16),
        pltpu.VMEM((3 * CL * YDIM, PTS), jnp.float32),
    ]
    if final is None:
        out_shape = jax.ShapeDtypeStruct(acc_shape, jnp.float32)
        out_specs = VMEM
    else:
        args += list(final)
        out_shape = [
            jax.ShapeDtypeStruct((CL, PTS), jnp.float32),
            jax.ShapeDtypeStruct((3 * BR_DEV, PTS), jnp.float32),
        ]
        out_specs = [VMEM] * 2
        scratch = [pltpu.VMEM(acc_shape, jnp.float32)] + scratch
    shape = tuple((slot, len(parts)) for slot, parts in blocks)
    return pl.pallas_call(
        functools.partial(ring_kernel, turn, shape, acc is not None, final is not None),
        out_shape=out_shape,
        in_specs=[SMEM] * 2 + [VMEM] * (len(args) - 2),
        out_specs=out_specs,
        scratch_shapes=scratch,
        compiler_params=pltpu.CompilerParams(vmem_limit_bytes=16 * 2**20),
        cost_estimate=pl.CostEstimate(
            flops=2 * 40 * PTS * 256 * 256, bytes_accessed=8 * 2**20, transcendentals=10**6
        ),
    )(*args)


def hop(block, distance):
    peers = lax.axis_size("tile")
    return lax.ppermute(block, "tile", [(i, (i + distance) % peers) for i in range(peers)])


def shifted(block, axis, distance):
    devices = range(lax.axis_size(axis))
    route = [(i - distance, i) for i in devices if i - distance in devices]
    return lax.ppermute(block, axis, route)


def local(
    history,
    positions,
    kappa_old,
    threshold,
    pair_ids,
    reader_counts,
    brick_map,
    strain_disp,
    couple,
):
    points = positions[0].transpose(1, 0, 2)
    own = jnp.concatenate(
        [history[0].reshape(HIST_ROWS, PTS), points.reshape(3 * CL, PTS)], axis=0
    )
    tile = lax.axis_index("tile")
    last = N_TILE // 2 - 1
    up, down = hop(own, 1), hop(own, -1)
    keys = pair_keys(pair_ids[0].T, reader_counts, tile)
    prepared = setup(keys, own)
    acc = None
    for s in range(1, last + 1):
        block = [(0, [up]), (1, [down])] + ([(2, [own])] if s <= OWN_ROUNDS else [])
        if acc is None:
            up, prepared = lax.optimization_barrier((up, prepared))
        else:
            up, acc = lax.optimization_barrier((up, acc))
        if s < last:
            up, down = hop(up, 1), hop(down, -1)
        else:
            far = hop(up, 1)
        acc = consume(prepared, s, block, acc)
    brick = brick_map - (tile - 1) * BR_DEV
    damage_here, shares = consume(
        prepared, last + 1, [(1, [far])], acc, (kappa_old[0], threshold[0], strain_disp, brick)
    )
    low, mid, top = shares[:BR_DEV], shares[BR_DEV : 2 * BR_DEV], shares[2 * BR_DEV :]
    force = mid + shifted(top, "tile", 1) + shifted(low, "tile", -1)
    before = shifted(force[-1:], "slab", 1)
    after = shifted(force[:1], "slab", -1)
    padded = jnp.concatenate([before, force, after], axis=0)
    residual_here = force + jnp.dot(
        padded[:-2] + padded[2:],
        couple,
        precision=lax.Precision.HIGHEST,
        preferred_element_type=jnp.float32,
    )
    return (damage_here[None], residual_here[:, None, :])


def solution(mesh):
    placed = (
        P("slab", "tile", None, None),
        P("slab", "tile", None, None),
        P("slab", "tile", None),
        P("slab", "tile", None),
        P("slab", "tile", None),
        P("slab", "tile"),
        P("slab", "tile"),
        P(),
        P(),
    )
    return jax.shard_map(
        local,
        mesh=mesh,
        in_specs=placed,
        out_specs=(P("slab", "tile", None), P("slab", "tile", None)),
        check_vma=False,
    )
```

```python
import functools
import math

import jax
import jax.numpy as jnp
from jax import lax
from jax.experimental import pallas as pl
from jax.experimental.pallas import tpu as pltpu
from jax.sharding import PartitionSpec as P

PTS = 128
COLS = 8
PAIRS = 8
CL = 128
BR_DEV = 32
N_TILE = 16
SHARP = 12.0
SOFTEN = 2.0
SCALE = SHARP * math.log2(math.e)

UNITS = 16
STEP = 2 * UNITS
ROUNDS = N_TILE // 2 + 1
REGION = CL * PAIRS
KEY_SHIFT = 20
OWN_ROUNDS = 3
YDIM = 8
KDIM = 2 * YDIM
HIST_ROWS = CL * COLS
ACC_ROWS = (CL + 1) * 2 * COLS
SMEM = pl.BlockSpec(memory_space=pltpu.SMEM)
VMEM = pl.BlockSpec(memory_space=pltpu.VMEM)


def split2(x):
    hi = x.astype(jnp.bfloat16).astype(jnp.float32)
    return hi, x - hi


def split3(x):
    hi, rest = split2(x)
    return (hi,) + split2(rest)


def reader_rows(here_ref, rows_ref):
    here = [
        here_ref[HIST_ROWS + k * CL : HIST_ROWS + (k + 1) * CL].astype(jnp.float32)
        for k in range(3)
    ]
    twice = [split2((2.0 * SCALE) * h) for h in here]
    norm = split2(-SCALE * (here[0] * here[0] + here[1] * here[1] + here[2] * here[2]))
    one = jnp.ones((CL, PTS), jnp.float32)
    none = jnp.zeros((CL, PTS), jnp.float32)
    rows = [twice[k][0] for k in range(3)] + [one] * 3 + [norm[0], none]
    rows += [twice[k][1] for k in range(3)] + [none] * 3 + [norm[1], none]
    for k, row in enumerate(rows):
        rows_ref[pl.ds(k, CL, stride=KDIM), :] = row


def turn_rows(g, rows_ref, x_ref):
    four = [rows_ref[pl.ds(pl.multiple_of((g * 4 + m) * KDIM, KDIM), KDIM), :] for m in range(4)]
    turned = jnp.concatenate([f for f in four for _ in range(2)], axis=0).T
    turned = turned.astype(jnp.bfloat16)
    for m in range(4):
        x_ref[g * 4 + m] = turned[:, m * 2 * KDIM : (m + 1) * 2 * KDIM]


def setup_kernel(
    key_ref, here_ref, list_ref, bounds_ref, x_ref, low_ref, high_ref, rows_ref
):
    reader_rows(here_ref, rows_ref)
    for k in range(ROUNDS):
        low_ref[k] = k * REGION + REGION // 2
        high_ref[k] = k * REGION + REGION // 2

    def sixteen(i, carry):
        for u in range(4):
            turn_rows(i * 4 + u, rows_ref, x_ref)
        for u in range(8):
            for p in range(PAIRS):
                key = key_ref[p, i * 8 + u]
                k = key >> KEY_SHIFT
                at = low_ref[k] - 1
                list_ref[at] = key & ((1 << KEY_SHIFT) - 1)
                low_ref[k] = at
                key = key_ref[p, CL // 2 + i * 8 + u]
                k = key >> KEY_SHIFT
                at = high_ref[k]
                list_ref[at] = key & ((1 << KEY_SHIFT) - 1)
                high_ref[k] = at + 1
        return carry

    lax.fori_loop(0, CL // 16, sixteen, 0)
    for k in range(ROUNDS):
        bounds_ref[k] = low_ref[k]
        bounds_ref[ROUNDS + k] = high_ref[k]


def setup(keys, own):
    return pl.pallas_call(
        setup_kernel,
        out_shape=[
            jax.ShapeDtypeStruct((ROUNDS * REGION + STEP,), jnp.int32),
            jax.ShapeDtypeStruct((2 * ROUNDS,), jnp.int32),
            jax.ShapeDtypeStruct((CL, PTS, 2 * KDIM), jnp.bfloat16),
        ],
        in_specs=[SMEM, VMEM],
        out_specs=[SMEM] * 2 + [VMEM],
        scratch_shapes=[
            pltpu.SMEM((ROUNDS,), jnp.int32),
            pltpu.SMEM((ROUNDS,), jnp.int32),
            pltpu.VMEM((CL * KDIM, PTS), jnp.float32),
        ],
        compiler_params=pltpu.CompilerParams(vmem_limit_bytes=16 * 2**20),
        cost_estimate=pl.CostEstimate(flops=10**6, bytes_accessed=10**7, transcendentals=0),
    )(keys, own)


def pair_keys(ids, counts, tile):
    reader = lax.broadcasted_iota(jnp.int32, ids.shape, 1)
    entry = lax.broadcasted_iota(jnp.int32, ids.shape, 0)
    ahead = ((ids >> 7) - tile) & (N_TILE - 1)
    near = jnp.minimum(ahead, N_TILE - ahead)
    own = ahead == 0
    slot = jnp.where(own, 2, jnp.where(ahead == near, 1, 0))
    turn = jnp.where(own, 1 + lax.rem(reader, OWN_ROUNDS), near)
    turn = jnp.where(entry < counts, turn, 0)
    return (turn << KEY_SHIFT) | (reader << 9) | (slot << 7) | (ids & (CL - 1))


def source_rows(block, spots, y_ref):
    norm = spots[0] * spots[0] + spots[1] * spots[1] + spots[2] * spots[2]
    one = jnp.ones((CL, PTS), jnp.float32)
    rows = spots + list(split3(-SCALE * norm)) + [one, 0.0 * one]
    for k, row in enumerate(rows):
        y_ref[pl.ds(block * (CL * YDIM) + k, CL, stride=YDIM), :] = row


def pairs(start, end, list_s, x_ref, hist_ref, y_ref, acc_ref):
    first = lax.broadcasted_iota(jnp.int32, (PTS, 2 * KDIM), 1) < KDIM
    zero_y = jnp.zeros((KDIM, PTS), jnp.float32)
    zero_h = jnp.zeros((COLS, PTS), jnp.float32)
    row = lax.broadcasted_iota(jnp.int32, (2 * COLS, 2 * PTS), 0) >> 3
    side = lax.broadcasted_iota(jnp.int32, (2 * COLS, 2 * PTS), 1) >> 7
    ones = (row == side).astype(jnp.float32).astype(jnp.bfloat16)

    def beside(one, other, zero):
        top = jnp.concatenate([one, zero], axis=1)
        bottom = jnp.concatenate([zero, other], axis=1)
        return jnp.concatenate([top, bottom], axis=0).astype(jnp.bfloat16)

    def source_points(q):
        y = y_ref[pl.ds(pl.multiple_of(q * YDIM, YDIM), YDIM), :]
        return jnp.concatenate([y, y], axis=0)

    def source_hist(q):
        at = pl.multiple_of((q >> 1) * (2 * COLS), 2 * COLS)
        two = hist_ref[pl.ds(at, 2 * COLS), :].astype(jnp.float32)
        return jnp.where((q & 1) == 1, two[COLS:], two[:COLS])

    def step(i, carry):
        at = start + i * STEP
        unused = (CL << 9) | CL
        entries = [jnp.where(at + k < end, list_s[at + k], unused) for k in range(STEP)]
        readers = [e >> 9 for e in entries]
        sources = [e & (4 * CL - 1) for e in entries]
        both = [(2 * u, 2 * u + 1) for u in range(UNITS)]
        weights = []
        for a, b in both:
            lhs = jnp.where(first, x_ref[readers[a] & (CL - 1)], x_ref[readers[b] & (CL - 1)])
            rhs = beside(source_points(sources[a]), source_points(sources[b]), zero_y)
            power = jnp.dot(lhs, rhs, preferred_element_type=jnp.float32)
            weights.append(jnp.exp2(power).astype(jnp.bfloat16))
        outs = []
        for (a, b), weight in zip(both, weights):
            hist = beside(source_hist(sources[a]), source_hist(sources[b]), zero_h)
            outs.append(
                lax.dot_general(
                    jnp.concatenate([hist, ones], axis=0),
                    weight,
                    (((1,), (1,)), ((), ())),
                    preferred_element_type=jnp.float32,
                )
            )
        for unit, out in zip(both, outs):
            for half in range(2):
                at = pl.multiple_of(readers[unit[half]] * (2 * COLS), 2 * COLS)
                acc_ref[pl.ds(at, COLS), :] += out[half * COLS : (half + 1) * COLS]
                acc_ref[pl.ds(at + COLS, COLS), :] += out[(2 + half) * COLS : (3 + half) * COLS]
        return carry

    lax.fori_loop(0, (end - start + (STEP - 1)) >> 5, step, 0)


def prepare(slot, parts, hist_ref, y_ref):
    at = 0
    spots = []
    for part in parts:
        rows = part.shape[0]
        take = min(rows, HIST_ROWS - at)
        if take > 0:
            base = slot * HIST_ROWS + at
            hist_ref[base : base + take] = part[:take]
            at += take
        for k in range(max(take, 0), rows, CL):
            spots.append(part[k : k + CL].astype(jnp.float32))
    source_rows(slot, spots, y_ref)


def finish(acc_ref, kappa_ref, threshold_ref, disp_ref, brick_ref, damage_ref, shares_ref):
    inverse = 1.0 / acc_ref[pl.ds(COLS, CL, stride=2 * COLS), :]
    threshold = threshold_ref[...]
    strain = acc_ref[pl.ds(0, CL, stride=2 * COLS), :] * inverse
    kappa = jnp.maximum(jnp.maximum(kappa_ref[...], strain), threshold)
    damage = 1.0 - (threshold / kappa) * jnp.exp(-(kappa - threshold) / SOFTEN)
    damage_ref[...] = damage
    left = 1.0 - damage
    term = jnp.zeros((CL, PTS), jnp.float32)
    for c in range(COLS):
        mean = acc_ref[pl.ds(c, CL, stride=2 * COLS), :] * inverse
        term = term + jnp.dot(
            (left * mean).astype(jnp.bfloat16),
            disp_ref[c * PTS : (c + 1) * PTS, :],
            preferred_element_type=jnp.float32,
        )
    rows = lax.broadcasted_iota(jnp.int32, (3 * BR_DEV, CL), 0)
    onehot = (rows == brick_ref[...]).astype(jnp.float32)
    shares_ref[...] = jnp.dot(
        onehot, term, precision=lax.Precision.HIGHEST, preferred_element_type=jnp.float32
    )


def ring_kernel(turn, shape, has_acc, final, *refs):
    refs = list(refs)
    take = lambda n: [refs.pop(0) for _ in range(n)]
    bounds_s, list_s, x_ref = take(3)
    blocks = [(slot, take(n)) for slot, n in shape]
    acc_in = take(1)[0] if has_acc else None
    final_in = take(4) if final else None
    final_out = take(2) if final else None
    acc_ref, hist_ref, y_ref = take(3)
    acc_ref[...] = acc_in[...] if has_acc else jnp.zeros_like(acc_ref)
    for slot, parts in blocks:
        prepare(slot, parts, hist_ref, y_ref)
    skip = turn * REGION
    start, end = bounds_s[turn] - skip, bounds_s[ROUNDS + turn] - skip
    pairs(start, end, list_s, x_ref, hist_ref, y_ref, acc_ref)
    if final:
        finish(acc_ref, *final_in, *final_out)


def consume(prepared, turn, blocks, acc, final=None):
    lists, bounds, x_rows = prepared
    lists = lists[turn * REGION : (turn + 1) * REGION + STEP]
    args = [bounds, lists, x_rows] + [part for _, parts in blocks for part in parts]
    if acc is not None:
        args.append(acc)
    acc_shape = (ACC_ROWS, PTS)
    scratch = [
        pltpu.VMEM((3 * HIST_ROWS, PTS), jnp.bfloat16),
        pltpu.VMEM((3 * CL * YDIM, PTS), jnp.float32),
    ]
    if final is None:
        out_shape = jax.ShapeDtypeStruct(acc_shape, jnp.float32)
        out_specs = VMEM
    else:
        args += list(final)
        out_shape = [
            jax.ShapeDtypeStruct((CL, PTS), jnp.float32),
            jax.ShapeDtypeStruct((3 * BR_DEV, PTS), jnp.float32),
        ]
        out_specs = [VMEM] * 2
        scratch = [pltpu.VMEM(acc_shape, jnp.float32)] + scratch
    shape = tuple((slot, len(parts)) for slot, parts in blocks)
    return pl.pallas_call(
        functools.partial(ring_kernel, turn, shape, acc is not None, final is not None),
        out_shape=out_shape,
        in_specs=[SMEM] * 2 + [VMEM] * (len(args) - 2),
        out_specs=out_specs,
        scratch_shapes=scratch,
        compiler_params=pltpu.CompilerParams(vmem_limit_bytes=16 * 2**20),
        cost_estimate=pl.CostEstimate(
            flops=2 * 40 * PTS * 256 * 256, bytes_accessed=8 * 2**20, transcendentals=10**6
        ),
    )(*args)


def hop(block, distance):
    peers = lax.axis_size("tile")
    return lax.ppermute(block, "tile", [(i, (i + distance) % peers) for i in range(peers)])


def shifted(block, axis, distance):
    devices = range(lax.axis_size(axis))
    route = [(i - distance, i) for i in devices if i - distance in devices]
    return lax.ppermute(block, axis, route)


def local(
    history,
    positions,
    kappa_old,
    threshold,
    pair_ids,
    reader_counts,
    brick_map,
    strain_disp,
    couple,
):
    points = positions[0].transpose(1, 0, 2)
    own = jnp.concatenate(
        [history[0].reshape(HIST_ROWS, PTS), points.reshape(3 * CL, PTS)], axis=0
    )
    tile = lax.axis_index("tile")
    last = N_TILE // 2 - 1
    up, down = hop(own, 1), hop(own, -1)
    keys = pair_keys(pair_ids[0].T, reader_counts, tile)
    prepared = setup(keys, own)
    acc = None
    for s in range(1, last + 1):
        block = [(0, [up]), (1, [down])] + ([(2, [own])] if s <= OWN_ROUNDS else [])
        if acc is None:
            up, prepared = lax.optimization_barrier((up, prepared))
        else:
            up, acc = lax.optimization_barrier((up, acc))
        if s < last:
            up, down = hop(up, 1), hop(down, -1)
        else:
            far = hop(up, 1)
        acc = consume(prepared, s, block, acc)
    brick = brick_map - (tile - 1) * BR_DEV
    damage_here, shares = consume(
        prepared, last + 1, [(1, [far])], acc, (kappa_old[0], threshold[0], strain_disp, brick)
    )
    low, mid, top = shares[:BR_DEV], shares[BR_DEV : 2 * BR_DEV], shares[2 * BR_DEV :]
    force = mid + shifted(top, "tile", 1) + shifted(low, "tile", -1)
    before = shifted(force[-1:], "slab", 1)
    after = shifted(force[:1], "slab", -1)
    padded = jnp.concatenate([before, force, after], axis=0)
    residual_here = force + jnp.dot(
        padded[:-2] + padded[2:],
        couple,
        precision=lax.Precision.HIGHEST,
        preferred_element_type=jnp.float32,
    )
    return (damage_here[None], residual_here[:, None, :])


def solution(mesh):
    placed = (
        P("slab", "tile", None, None),
        P("slab", "tile", None, None),
        P("slab", "tile", None),
        P("slab", "tile", None),
        P("slab", "tile", None),
        P("slab", "tile"),
        P("slab", "tile"),
        P(),
        P(),
    )
    return jax.shard_map(
        local,
        mesh=mesh,
        in_specs=placed,
        out_specs=(P("slab", "tile", None), P("slab", "tile", None)),
        check_vma=False,
    )
```

```python
import functools
import math

import jax
import jax.numpy as jnp
from jax import lax
from jax.experimental import pallas as pl
from jax.experimental.pallas import tpu as pltpu
from jax.sharding import PartitionSpec as P

PTS = 128
COLS = 8
PAIRS = 8
CL = 128
BR_DEV = 32
N_TILE = 16
SHARP = 12.0
SOFTEN = 2.0
SCALE = SHARP * math.log2(math.e)

UNITS = 16
STEP = 2 * UNITS
ROUNDS = N_TILE // 2 + 1
REGION = CL * PAIRS
KEY_SHIFT = 20
OWN_ROUNDS = 3
YDIM = 8
KDIM = 2 * YDIM
HIST_ROWS = CL * COLS
ACC_ROWS = (CL + 1) * 2 * COLS
SMEM = pl.BlockSpec(memory_space=pltpu.SMEM)
VMEM = pl.BlockSpec(memory_space=pltpu.VMEM)


def split2(x):
    hi = x.astype(jnp.bfloat16).astype(jnp.float32)
    return hi, x - hi


def split3(x):
    hi, rest = split2(x)
    return (hi,) + split2(rest)


def reader_rows(here_ref, rows_ref):
    here = [
        here_ref[HIST_ROWS + k * CL : HIST_ROWS + (k + 1) * CL].astype(jnp.float32)
        for k in range(3)
    ]
    twice = [split2((2.0 * SCALE) * h) for h in here]
    norm = split2(-SCALE * (here[0] * here[0] + here[1] * here[1] + here[2] * here[2]))
    one = jnp.ones((CL, PTS), jnp.float32)
    none = jnp.zeros((CL, PTS), jnp.float32)
    rows = [twice[k][0] for k in range(3)] + [one] * 3 + [norm[0], none]
    rows += [twice[k][1] for k in range(3)] + [none] * 3 + [norm[1], none]
    for k, row in enumerate(rows):
        rows_ref[pl.ds(k, CL, stride=KDIM), :] = row


def turn_rows(g, rows_ref, x_ref):
    four = [rows_ref[pl.ds(pl.multiple_of((g * 4 + m) * KDIM, KDIM), KDIM), :] for m in range(4)]
    turned = jnp.concatenate([f for f in four for _ in range(2)], axis=0).T
    turned = turned.astype(jnp.bfloat16)
    for m in range(4):
        x_ref[g * 4 + m] = turned[:, m * 2 * KDIM : (m + 1) * 2 * KDIM]


def turn_kernel(here_ref, x_ref, rows_ref):
    reader_rows(here_ref, rows_ref)

    def sixteen(i, carry):
        for u in range(4):
            turn_rows(i * 4 + u, rows_ref, x_ref)
        return carry

    lax.fori_loop(0, CL // 16, sixteen, 0)


def list_kernel(key_ref, list_ref, bounds_ref, low_ref, high_ref):
    for k in range(ROUNDS):
        low_ref[k] = k * REGION + REGION // 2
        high_ref[k] = k * REGION + REGION // 2

    def sixteen(i, carry):
        for u in range(8):
            for p in range(PAIRS):
                key = key_ref[p, i * 8 + u]
                k = key >> KEY_SHIFT
                at = low_ref[k] - 1
                list_ref[at] = key & ((1 << KEY_SHIFT) - 1)
                low_ref[k] = at
                key = key_ref[p, CL // 2 + i * 8 + u]
                k = key >> KEY_SHIFT
                at = high_ref[k]
                list_ref[at] = key & ((1 << KEY_SHIFT) - 1)
                high_ref[k] = at + 1
        return carry

    lax.fori_loop(0, CL // 16, sixteen, 0)
    for k in range(ROUNDS):
        bounds_ref[k] = low_ref[k]
        bounds_ref[ROUNDS + k] = high_ref[k]


def make_lists(keys):
    return pl.pallas_call(
        list_kernel,
        out_shape=[
            jax.ShapeDtypeStruct((ROUNDS * REGION + STEP,), jnp.int32),
            jax.ShapeDtypeStruct((2 * ROUNDS,), jnp.int32),
        ],
        in_specs=[SMEM],
        out_specs=[SMEM] * 2,
        scratch_shapes=[pltpu.SMEM((ROUNDS,), jnp.int32), pltpu.SMEM((ROUNDS,), jnp.int32)],
        cost_estimate=pl.CostEstimate(flops=10**6, bytes_accessed=10**7, transcendentals=0),
    )(keys)


def turned_rows(own):
    return pl.pallas_call(
        turn_kernel,
        out_shape=jax.ShapeDtypeStruct((CL, PTS, 2 * KDIM), jnp.bfloat16),
        in_specs=[VMEM],
        out_specs=VMEM,
        scratch_shapes=[pltpu.VMEM((CL * KDIM, PTS), jnp.float32)],
        compiler_params=pltpu.CompilerParams(vmem_limit_bytes=16 * 2**20),
        cost_estimate=pl.CostEstimate(flops=10**6, bytes_accessed=10**7, transcendentals=0),
    )(own)


def pair_keys(ids, counts, tile):
    reader = lax.broadcasted_iota(jnp.int32, ids.shape, 1)
    entry = lax.broadcasted_iota(jnp.int32, ids.shape, 0)
    ahead = ((ids >> 7) - tile) & (N_TILE - 1)
    near = jnp.minimum(ahead, N_TILE - ahead)
    own = ahead == 0
    slot = jnp.where(own, 2, jnp.where(ahead == near, 1, 0))
    turn = jnp.where(own, 1 + lax.rem(reader, OWN_ROUNDS), near)
    turn = jnp.where(entry < counts, turn, 0)
    return (turn << KEY_SHIFT) | (reader << 9) | (slot << 7) | (ids & (CL - 1))


def source_rows(block, spots, y_ref):
    norm = spots[0] * spots[0] + spots[1] * spots[1] + spots[2] * spots[2]
    one = jnp.ones((CL, PTS), jnp.float32)
    rows = spots + list(split3(-SCALE * norm)) + [one, 0.0 * one]
    for k, row in enumerate(rows):
        y_ref[pl.ds(block * (CL * YDIM) + k, CL, stride=YDIM), :] = row


def pairs(start, end, list_s, x_ref, hist_ref, y_ref, acc_ref):
    first = lax.broadcasted_iota(jnp.int32, (PTS, 2 * KDIM), 1) < KDIM
    zero_y = jnp.zeros((KDIM, PTS), jnp.float32)
    zero_h = jnp.zeros((COLS, PTS), jnp.float32)
    row = lax.broadcasted_iota(jnp.int32, (2 * COLS, 2 * PTS), 0) >> 3
    side = lax.broadcasted_iota(jnp.int32, (2 * COLS, 2 * PTS), 1) >> 7
    ones = (row == side).astype(jnp.float32).astype(jnp.bfloat16)

    def beside(one, other, zero):
        top = jnp.concatenate([one, zero], axis=1)
        bottom = jnp.concatenate([zero, other], axis=1)
        return jnp.concatenate([top, bottom], axis=0).astype(jnp.bfloat16)

    def source_points(q):
        y = y_ref[pl.ds(pl.multiple_of(q * YDIM, YDIM), YDIM), :]
        return jnp.concatenate([y, y], axis=0)

    def source_hist(q):
        at = pl.multiple_of((q >> 1) * (2 * COLS), 2 * COLS)
        two = hist_ref[pl.ds(at, 2 * COLS), :].astype(jnp.float32)
        return jnp.where((q & 1) == 1, two[COLS:], two[:COLS])

    def step(i, carry):
        at = start + i * STEP
        unused = (CL << 9) | CL
        entries = [jnp.where(at + k < end, list_s[at + k], unused) for k in range(STEP)]
        readers = [e >> 9 for e in entries]
        sources = [e & (4 * CL - 1) for e in entries]
        both = [(2 * u, 2 * u + 1) for u in range(UNITS)]
        weights = []
        for a, b in both:
            lhs = jnp.where(first, x_ref[readers[a] & (CL - 1)], x_ref[readers[b] & (CL - 1)])
            rhs = beside(source_points(sources[a]), source_points(sources[b]), zero_y)
            power = jnp.dot(lhs, rhs, preferred_element_type=jnp.float32)
            weights.append(jnp.exp2(power).astype(jnp.bfloat16))
        outs = []
        for (a, b), weight in zip(both, weights):
            hist = beside(source_hist(sources[a]), source_hist(sources[b]), zero_h)
            outs.append(
                lax.dot_general(
                    jnp.concatenate([hist, ones], axis=0),
                    weight,
                    (((1,), (1,)), ((), ())),
                    preferred_element_type=jnp.float32,
                )
            )
        for unit, out in zip(both, outs):
            for half in range(2):
                at = pl.multiple_of(readers[unit[half]] * (2 * COLS), 2 * COLS)
                acc_ref[pl.ds(at, COLS), :] += out[half * COLS : (half + 1) * COLS]
                acc_ref[pl.ds(at + COLS, COLS), :] += out[(2 + half) * COLS : (3 + half) * COLS]
        return carry

    lax.fori_loop(0, (end - start + (STEP - 1)) >> 5, step, 0)


def prepare(slot, parts, hist_ref, y_ref):
    at = 0
    spots = []
    for part in parts:
        rows = part.shape[0]
        take = min(rows, HIST_ROWS - at)
        if take > 0:
            base = slot * HIST_ROWS + at
            hist_ref[base : base + take] = part[:take]
            at += take
        for k in range(max(take, 0), rows, CL):
            spots.append(part[k : k + CL].astype(jnp.float32))
    source_rows(slot, spots, y_ref)


def finish(acc_ref, kappa_ref, threshold_ref, disp_ref, brick_ref, damage_ref, shares_ref):
    inverse = 1.0 / acc_ref[pl.ds(COLS, CL, stride=2 * COLS), :]
    threshold = threshold_ref[...]
    strain = acc_ref[pl.ds(0, CL, stride=2 * COLS), :] * inverse
    kappa = jnp.maximum(jnp.maximum(kappa_ref[...], strain), threshold)
    damage = 1.0 - (threshold / kappa) * jnp.exp(-(kappa - threshold) / SOFTEN)
    damage_ref[...] = damage
    left = 1.0 - damage
    term = jnp.zeros((CL, PTS), jnp.float32)
    for c in range(COLS):
        mean = acc_ref[pl.ds(c, CL, stride=2 * COLS), :] * inverse
        term = term + jnp.dot(
            (left * mean).astype(jnp.bfloat16),
            disp_ref[c * PTS : (c + 1) * PTS, :],
            preferred_element_type=jnp.float32,
        )
    rows = lax.broadcasted_iota(jnp.int32, (3 * BR_DEV, CL), 0)
    onehot = (rows == brick_ref[...]).astype(jnp.float32)
    shares_ref[...] = jnp.dot(
        onehot, term, precision=lax.Precision.HIGHEST, preferred_element_type=jnp.float32
    )


def ring_kernel(turn, shape, has_acc, final, *refs):
    refs = list(refs)
    take = lambda n: [refs.pop(0) for _ in range(n)]
    bounds_s, list_s, x_ref = take(3)
    blocks = [(slot, take(n)) for slot, n in shape]
    acc_in = take(1)[0] if has_acc else None
    final_in = take(4) if final else None
    final_out = take(2) if final else None
    acc_ref, hist_ref, y_ref = take(3)
    acc_ref[...] = acc_in[...] if has_acc else jnp.zeros_like(acc_ref)
    for slot, parts in blocks:
        prepare(slot, parts, hist_ref, y_ref)
    skip = turn * REGION
    start, end = bounds_s[turn] - skip, bounds_s[ROUNDS + turn] - skip
    pairs(start, end, list_s, x_ref, hist_ref, y_ref, acc_ref)
    if final:
        finish(acc_ref, *final_in, *final_out)


def consume(prepared, turn, blocks, acc, final=None):
    lists, bounds, x_rows = prepared
    lists = lists[turn * REGION : (turn + 1) * REGION + STEP]
    args = [bounds, lists, x_rows] + [part for _, parts in blocks for part in parts]
    if acc is not None:
        args.append(acc)
    acc_shape = (ACC_ROWS, PTS)
    scratch = [
        pltpu.VMEM((3 * HIST_ROWS, PTS), jnp.bfloat16),
        pltpu.VMEM((3 * CL * YDIM, PTS), jnp.float32),
    ]
    if final is None:
        out_shape = jax.ShapeDtypeStruct(acc_shape, jnp.float32)
        out_specs = VMEM
    else:
        args += list(final)
        out_shape = [
            jax.ShapeDtypeStruct((CL, PTS), jnp.float32),
            jax.ShapeDtypeStruct((3 * BR_DEV, PTS), jnp.float32),
        ]
        out_specs = [VMEM] * 2
        scratch = [pltpu.VMEM(acc_shape, jnp.float32)] + scratch
    shape = tuple((slot, len(parts)) for slot, parts in blocks)
    return pl.pallas_call(
        functools.partial(ring_kernel, turn, shape, acc is not None, final is not None),
        out_shape=out_shape,
        in_specs=[SMEM] * 2 + [VMEM] * (len(args) - 2),
        out_specs=out_specs,
        scratch_shapes=scratch,
        compiler_params=pltpu.CompilerParams(vmem_limit_bytes=16 * 2**20),
        cost_estimate=pl.CostEstimate(
            flops=2 * 40 * PTS * 256 * 256, bytes_accessed=8 * 2**20, transcendentals=10**6
        ),
    )(*args)


def hop(block, distance):
    peers = lax.axis_size("tile")
    return lax.ppermute(block, "tile", [(i, (i + distance) % peers) for i in range(peers)])


def shifted(block, axis, distance):
    devices = range(lax.axis_size(axis))
    route = [(i - distance, i) for i in devices if i - distance in devices]
    return lax.ppermute(block, axis, route)


def local(
    history,
    positions,
    kappa_old,
    threshold,
    pair_ids,
    reader_counts,
    brick_map,
    strain_disp,
    couple,
):
    points = positions[0].transpose(1, 0, 2)
    own = jnp.concatenate(
        [history[0].reshape(HIST_ROWS, PTS), points.reshape(3 * CL, PTS)], axis=0
    )
    tile = lax.axis_index("tile")
    last = N_TILE // 2 - 1
    up, down = hop(own, 1), hop(own, -1)
    keys = pair_keys(pair_ids[0].T, reader_counts, tile)
    lists = make_lists(keys)
    acc = None
    blocks = {}
    for s in range(1, last + 1):
        blocks[s] = [(0, [up]), (1, [down])] + ([(2, [own])] if s <= OWN_ROUNDS else [])
        if s == 1:
            up, lists, later = lax.optimization_barrier((up, lists, own))
            x_rows = turned_rows(later)
        elif s == 2:
            up, x_rows = lax.optimization_barrier((up, x_rows))
        else:
            acc = consume((*lists, x_rows), s - 2, blocks[s - 2], acc)
            up, acc = lax.optimization_barrier((up, acc))
        if s < last:
            up, down = hop(up, 1), hop(down, -1)
        else:
            far = hop(up, 1)
    prepared = (*lists, x_rows)
    for s in (last - 1, last):
        acc = consume(prepared, s, blocks[s], acc)
    brick = brick_map - (tile - 1) * BR_DEV
    damage_here, shares = consume(
        prepared, last + 1, [(1, [far])], acc, (kappa_old[0], threshold[0], strain_disp, brick)
    )
    low, mid, top = shares[:BR_DEV], shares[BR_DEV : 2 * BR_DEV], shares[2 * BR_DEV :]
    force = mid + shifted(top, "tile", 1) + shifted(low, "tile", -1)
    before = shifted(force[-1:], "slab", 1)
    after = shifted(force[:1], "slab", -1)
    padded = jnp.concatenate([before, force, after], axis=0)
    residual_here = force + jnp.dot(
        padded[:-2] + padded[2:],
        couple,
        precision=lax.Precision.HIGHEST,
        preferred_element_type=jnp.float32,
    )
    return (damage_here[None], residual_here[:, None, :])


def solution(mesh):
    placed = (
        P("slab", "tile", None, None),
        P("slab", "tile", None, None),
        P("slab", "tile", None),
        P("slab", "tile", None),
        P("slab", "tile", None),
        P("slab", "tile"),
        P("slab", "tile"),
        P(),
        P(),
    )
    return jax.shard_map(
        local,
        mesh=mesh,
        in_specs=placed,
        out_specs=(P("slab", "tile", None), P("slab", "tile", None)),
        check_vma=False,
    )
```

```python
import functools
import math

import jax
import jax.numpy as jnp
from jax import lax
from jax.experimental import pallas as pl
from jax.experimental.pallas import tpu as pltpu
from jax.sharding import PartitionSpec as P

PTS = 128
COLS = 8
PAIRS = 8
CL = 128
BR_DEV = 32
N_TILE = 16
SHARP = 12.0
SOFTEN = 2.0
SCALE = SHARP * math.log2(math.e)

UNITS = 16
STEP = 2 * UNITS
ROUNDS = N_TILE // 2 + 1
REGION = CL * PAIRS
KEY_SHIFT = 20
OWN_ROUNDS = 4
YDIM = 8
KDIM = 2 * YDIM
HIST_ROWS = CL * COLS
ACC_ROWS = (CL + 1) * 2 * COLS
SMEM = pl.BlockSpec(memory_space=pltpu.SMEM)
VMEM = pl.BlockSpec(memory_space=pltpu.VMEM)


def split2(x):
    hi = x.astype(jnp.bfloat16).astype(jnp.float32)
    return hi, x - hi


def split3(x):
    hi, rest = split2(x)
    return (hi,) + split2(rest)


def reader_rows(here_ref, rows_ref):
    here = [
        here_ref[HIST_ROWS + k * CL : HIST_ROWS + (k + 1) * CL].astype(jnp.float32)
        for k in range(3)
    ]
    twice = [split2((2.0 * SCALE) * h) for h in here]
    norm = split2(-SCALE * (here[0] * here[0] + here[1] * here[1] + here[2] * here[2]))
    one = jnp.ones((CL, PTS), jnp.float32)
    none = jnp.zeros((CL, PTS), jnp.float32)
    rows = [twice[k][0] for k in range(3)] + [one] * 3 + [norm[0], none]
    rows += [twice[k][1] for k in range(3)] + [none] * 3 + [norm[1], none]
    for k, row in enumerate(rows):
        rows_ref[pl.ds(k, CL, stride=KDIM), :] = row


def turn_rows(g, rows_ref, x_ref):
    four = [rows_ref[pl.ds(pl.multiple_of((g * 4 + m) * KDIM, KDIM), KDIM), :] for m in range(4)]
    turned = jnp.concatenate([f for f in four for _ in range(2)], axis=0).T
    turned = turned.astype(jnp.bfloat16)
    for m in range(4):
        x_ref[g * 4 + m] = turned[:, m * 2 * KDIM : (m + 1) * 2 * KDIM]


def turn_kernel(here_ref, x_ref, rows_ref):
    reader_rows(here_ref, rows_ref)

    def sixteen(i, carry):
        for u in range(4):
            turn_rows(i * 4 + u, rows_ref, x_ref)
        return carry

    lax.fori_loop(0, CL // 16, sixteen, 0)


def list_kernel(key_ref, list_ref, bounds_ref, low_ref, high_ref):
    for k in range(ROUNDS):
        low_ref[k] = k * REGION + REGION // 2
        high_ref[k] = k * REGION + REGION // 2

    def sixteen(i, carry):
        for u in range(8):
            for p in range(PAIRS):
                key = key_ref[p, i * 8 + u]
                k = key >> KEY_SHIFT
                at = low_ref[k] - 1
                list_ref[at] = key & ((1 << KEY_SHIFT) - 1)
                low_ref[k] = at
                key = key_ref[p, CL // 2 + i * 8 + u]
                k = key >> KEY_SHIFT
                at = high_ref[k]
                list_ref[at] = key & ((1 << KEY_SHIFT) - 1)
                high_ref[k] = at + 1
        return carry

    lax.fori_loop(0, CL // 16, sixteen, 0)
    for k in range(ROUNDS):
        bounds_ref[k] = low_ref[k]
        bounds_ref[ROUNDS + k] = high_ref[k]


def make_lists(keys):
    return pl.pallas_call(
        list_kernel,
        out_shape=[
            jax.ShapeDtypeStruct((ROUNDS * REGION + STEP,), jnp.int32),
            jax.ShapeDtypeStruct((2 * ROUNDS,), jnp.int32),
        ],
        in_specs=[SMEM],
        out_specs=[SMEM] * 2,
        scratch_shapes=[pltpu.SMEM((ROUNDS,), jnp.int32), pltpu.SMEM((ROUNDS,), jnp.int32)],
        cost_estimate=pl.CostEstimate(flops=10**6, bytes_accessed=10**7, transcendentals=0),
    )(keys)


def turned_rows(own):
    return pl.pallas_call(
        turn_kernel,
        out_shape=jax.ShapeDtypeStruct((CL, PTS, 2 * KDIM), jnp.bfloat16),
        in_specs=[VMEM],
        out_specs=VMEM,
        scratch_shapes=[pltpu.VMEM((CL * KDIM, PTS), jnp.float32)],
        compiler_params=pltpu.CompilerParams(vmem_limit_bytes=16 * 2**20),
        cost_estimate=pl.CostEstimate(flops=10**6, bytes_accessed=10**7, transcendentals=0),
    )(own)


def pair_keys(ids, counts, tile):
    reader = lax.broadcasted_iota(jnp.int32, ids.shape, 1)
    entry = lax.broadcasted_iota(jnp.int32, ids.shape, 0)
    ahead = ((ids >> 7) - tile) & (N_TILE - 1)
    near = jnp.minimum(ahead, N_TILE - ahead)
    own = ahead == 0
    slot = jnp.where(own, 2, jnp.where(ahead == near, 1, 0))
    turn = jnp.where(own, 1 + lax.rem(reader, OWN_ROUNDS), near)
    turn = jnp.where(entry < counts, turn, 0)
    return (turn << KEY_SHIFT) | (reader << 9) | (slot << 7) | (ids & (CL - 1))


def source_rows(block, spots, y_ref):
    norm = spots[0] * spots[0] + spots[1] * spots[1] + spots[2] * spots[2]
    one = jnp.ones((CL, PTS), jnp.float32)
    rows = spots + list(split3(-SCALE * norm)) + [one, 0.0 * one]
    for k, row in enumerate(rows):
        y_ref[pl.ds(block * (CL * YDIM) + k, CL, stride=YDIM), :] = row


def pairs(start, end, list_s, x_ref, hist_ref, y_ref, acc_ref):
    first = lax.broadcasted_iota(jnp.int32, (PTS, 2 * KDIM), 1) < KDIM
    zero_y = jnp.zeros((KDIM, PTS), jnp.float32)
    zero_h = jnp.zeros((COLS, PTS), jnp.float32)
    row = lax.broadcasted_iota(jnp.int32, (2 * COLS, 2 * PTS), 0) >> 3
    side = lax.broadcasted_iota(jnp.int32, (2 * COLS, 2 * PTS), 1) >> 7
    ones = (row == side).astype(jnp.float32).astype(jnp.bfloat16)

    def beside(one, other, zero):
        top = jnp.concatenate([one, zero], axis=1)
        bottom = jnp.concatenate([zero, other], axis=1)
        return jnp.concatenate([top, bottom], axis=0).astype(jnp.bfloat16)

    def source_points(q):
        y = y_ref[pl.ds(pl.multiple_of(q * YDIM, YDIM), YDIM), :]
        return jnp.concatenate([y, y], axis=0)

    def source_hist(q):
        at = pl.multiple_of((q >> 1) * (2 * COLS), 2 * COLS)
        two = hist_ref[pl.ds(at, 2 * COLS), :].astype(jnp.float32)
        return jnp.where((q & 1) == 1, two[COLS:], two[:COLS])

    def step(i, carry):
        at = start + i * STEP
        unused = (CL << 9) | CL
        entries = [jnp.where(at + k < end, list_s[at + k], unused) for k in range(STEP)]
        readers = [e >> 9 for e in entries]
        sources = [e & (4 * CL - 1) for e in entries]
        both = [(2 * u, 2 * u + 1) for u in range(UNITS)]
        weights = []
        for a, b in both:
            lhs = jnp.where(first, x_ref[readers[a] & (CL - 1)], x_ref[readers[b] & (CL - 1)])
            rhs = beside(source_points(sources[a]), source_points(sources[b]), zero_y)
            power = jnp.dot(lhs, rhs, preferred_element_type=jnp.float32)
            weights.append(jnp.exp2(power).astype(jnp.bfloat16))
        outs = []
        for (a, b), weight in zip(both, weights):
            hist = beside(source_hist(sources[a]), source_hist(sources[b]), zero_h)
            outs.append(
                lax.dot_general(
                    jnp.concatenate([hist, ones], axis=0),
                    weight,
                    (((1,), (1,)), ((), ())),
                    preferred_element_type=jnp.float32,
                )
            )
        for unit, out in zip(both, outs):
            for half in range(2):
                at = pl.multiple_of(readers[unit[half]] * (2 * COLS), 2 * COLS)
                acc_ref[pl.ds(at, COLS), :] += out[half * COLS : (half + 1) * COLS]
                acc_ref[pl.ds(at + COLS, COLS), :] += out[(2 + half) * COLS : (3 + half) * COLS]
        return carry

    lax.fori_loop(0, (end - start + (STEP - 1)) >> 5, step, 0)


def prepare(slot, parts, hist_ref, y_ref):
    at = 0
    spots = []
    for part in parts:
        rows = part.shape[0]
        take = min(rows, HIST_ROWS - at)
        if take > 0:
            base = slot * HIST_ROWS + at
            hist_ref[base : base + take] = part[:take]
            at += take
        for k in range(max(take, 0), rows, CL):
            spots.append(part[k : k + CL].astype(jnp.float32))
    source_rows(slot, spots, y_ref)


def finish(acc_ref, kappa_ref, threshold_ref, disp_ref, brick_ref, damage_ref, shares_ref):
    inverse = 1.0 / acc_ref[pl.ds(COLS, CL, stride=2 * COLS), :]
    threshold = threshold_ref[...]
    strain = acc_ref[pl.ds(0, CL, stride=2 * COLS), :] * inverse
    kappa = jnp.maximum(jnp.maximum(kappa_ref[...], strain), threshold)
    damage = 1.0 - (threshold / kappa) * jnp.exp(-(kappa - threshold) / SOFTEN)
    damage_ref[...] = damage
    left = 1.0 - damage
    term = jnp.zeros((CL, PTS), jnp.float32)
    for c in range(COLS):
        mean = acc_ref[pl.ds(c, CL, stride=2 * COLS), :] * inverse
        term = term + jnp.dot(
            (left * mean).astype(jnp.bfloat16),
            disp_ref[c * PTS : (c + 1) * PTS, :],
            preferred_element_type=jnp.float32,
        )
    rows = lax.broadcasted_iota(jnp.int32, (3 * BR_DEV, CL), 0)
    onehot = (rows == brick_ref[...]).astype(jnp.float32)
    shares_ref[...] = jnp.dot(
        onehot, term, precision=lax.Precision.HIGHEST, preferred_element_type=jnp.float32
    )


def ring_kernel(turn, shape, has_acc, final, *refs):
    refs = list(refs)
    take = lambda n: [refs.pop(0) for _ in range(n)]
    bounds_s, list_s, x_ref = take(3)
    blocks = [(slot, take(n)) for slot, n in shape]
    acc_in = take(1)[0] if has_acc else None
    final_in = take(4) if final else None
    final_out = take(2) if final else None
    acc_ref, hist_ref, y_ref = take(3)
    acc_ref[...] = acc_in[...] if has_acc else jnp.zeros_like(acc_ref)
    for slot, parts in blocks:
        prepare(slot, parts, hist_ref, y_ref)
    skip = turn * REGION
    start, end = bounds_s[turn] - skip, bounds_s[ROUNDS + turn] - skip
    pairs(start, end, list_s, x_ref, hist_ref, y_ref, acc_ref)
    if final:
        finish(acc_ref, *final_in, *final_out)


def consume(prepared, turn, blocks, acc, final=None):
    lists, bounds, x_rows = prepared
    lists = lists[turn * REGION : (turn + 1) * REGION + STEP]
    args = [bounds, lists, x_rows] + [part for _, parts in blocks for part in parts]
    if acc is not None:
        args.append(acc)
    acc_shape = (ACC_ROWS, PTS)
    scratch = [
        pltpu.VMEM((3 * HIST_ROWS, PTS), jnp.bfloat16),
        pltpu.VMEM((3 * CL * YDIM, PTS), jnp.float32),
    ]
    if final is None:
        out_shape = jax.ShapeDtypeStruct(acc_shape, jnp.float32)
        out_specs = VMEM
    else:
        args += list(final)
        out_shape = [
            jax.ShapeDtypeStruct((CL, PTS), jnp.float32),
            jax.ShapeDtypeStruct((3 * BR_DEV, PTS), jnp.float32),
        ]
        out_specs = [VMEM] * 2
        scratch = [pltpu.VMEM(acc_shape, jnp.float32)] + scratch
    shape = tuple((slot, len(parts)) for slot, parts in blocks)
    return pl.pallas_call(
        functools.partial(ring_kernel, turn, shape, acc is not None, final is not None),
        out_shape=out_shape,
        in_specs=[SMEM] * 2 + [VMEM] * (len(args) - 2),
        out_specs=out_specs,
        scratch_shapes=scratch,
        compiler_params=pltpu.CompilerParams(vmem_limit_bytes=16 * 2**20),
        cost_estimate=pl.CostEstimate(
            flops=2 * 40 * PTS * 256 * 256, bytes_accessed=8 * 2**20, transcendentals=10**6
        ),
    )(*args)


def hop(block, distance):
    peers = lax.axis_size("tile")
    return lax.ppermute(block, "tile", [(i, (i + distance) % peers) for i in range(peers)])


def shifted(block, axis, distance):
    devices = range(lax.axis_size(axis))
    route = [(i - distance, i) for i in devices if i - distance in devices]
    return lax.ppermute(block, axis, route)


def local(
    history,
    positions,
    kappa_old,
    threshold,
    pair_ids,
    reader_counts,
    brick_map,
    strain_disp,
    couple,
):
    points = positions[0].transpose(1, 0, 2)
    own = jnp.concatenate(
        [history[0].reshape(HIST_ROWS, PTS), points.reshape(3 * CL, PTS)], axis=0
    )
    tile = lax.axis_index("tile")
    last = N_TILE // 2 - 1
    up, down = hop(own, 1), hop(own, -1)
    keys = pair_keys(pair_ids[0].T, reader_counts, tile)
    lists = make_lists(keys)
    acc = None
    blocks = {}
    for s in range(1, last + 1):
        blocks[s] = [(0, [up]), (1, [down])] + ([(2, [own])] if s <= OWN_ROUNDS else [])
        if s == 1:
            up, lists, later = lax.optimization_barrier((up, lists, own))
            x_rows = turned_rows(later)
        elif s == 2:
            up, x_rows = lax.optimization_barrier((up, x_rows))
        else:
            acc = consume((*lists, x_rows), s - 2, blocks[s - 2], acc)
            up, acc = lax.optimization_barrier((up, acc))
        if s < last:
            up, down = hop(up, 1), hop(down, -1)
        else:
            far = hop(up, 1)
    prepared = (*lists, x_rows)
    for s in (last - 1, last):
        acc = consume(prepared, s, blocks[s], acc)
    brick = brick_map - (tile - 1) * BR_DEV
    damage_here, shares = consume(
        prepared, last + 1, [(1, [far])], acc, (kappa_old[0], threshold[0], strain_disp, brick)
    )
    low, mid, top = shares[:BR_DEV], shares[BR_DEV : 2 * BR_DEV], shares[2 * BR_DEV :]
    force = mid + shifted(top, "tile", 1) + shifted(low, "tile", -1)
    before = shifted(force[-1:], "slab", 1)
    after = shifted(force[:1], "slab", -1)
    padded = jnp.concatenate([before, force, after], axis=0)
    residual_here = force + jnp.dot(
        padded[:-2] + padded[2:],
        couple,
        precision=lax.Precision.HIGHEST,
        preferred_element_type=jnp.float32,
    )
    return (damage_here[None], residual_here[:, None, :])


def solution(mesh):
    placed = (
        P("slab", "tile", None, None),
        P("slab", "tile", None, None),
        P("slab", "tile", None),
        P("slab", "tile", None),
        P("slab", "tile", None),
        P("slab", "tile"),
        P("slab", "tile"),
        P(),
        P(),
    )
    return jax.shard_map(
        local,
        mesh=mesh,
        in_specs=placed,
        out_specs=(P("slab", "tile", None), P("slab", "tile", None)),
        check_vma=False,
    )
```
